256 devices in a mesh: row: 4 (over y_hi, core), col: 16 (over y_lo, z), tm: 4 (over x).
Axes of the slice: x: 4, y: 4 (y_hi: 2, y_lo: 2; y = y_hi * 2 + y_lo), z: 8, core: 2. Of those that a mesh axis runs over, the one named last changes fastest.
Arguments:
- traces: bfloat16 [2048, 128, 512], P(('row', 'col'), 'tm'), may hold values from -6 to 6
- live_flags: int32 [2048], P(('row', 'col')), may hold values 0 or 1
Outputs:
- stacks: bfloat16 [2048, 256, 256], P(('row', 'col', 'tm'))
The draws below stay inside these ranges and needn't reach their ends.
Inputs may be any that keep to these rules, and one draw needn't show every extreme that they name: `live_flags`: dead channels are 0, working ones 1.
All inputs are finite; a program needn't handle non-finite values. No bound on the sum of `live_flags` on one device may be relied on, other than what follows from the above.
Results may differ from the reference program's by a relative error of at most 0.006.
Values may be sent and summed in bfloat16 or wider, within the bound.
No kernel may reach another device: no remote copies, remote signals or barrier semaphores. Data moves between devices by JAX's collectives and lax.ppermute only.
A program may use at most 128 MiB of HBM per device.

```python
import jax
import jax.numpy as jnp
from jax import lax

NFFT = 512
OFFS = 256
LAGS = 256
SMOOTH = 32
CH_DEV = 32
CHANNELS = 2048
MINUTES = 128
N_ROW = 4
N_COL = 16


def with_ends(drawn, key, low, largest):
    spot = [jax.random.randint(jax.random.fold_in(key, axis), (), 0, length) for axis, length in enumerate(drawn.shape)]
    main_axis = drawn.shape.index(max(drawn.shape))
    neighbour = spot[:main_axis] + [(spot[main_axis] + 1) % drawn.shape[main_axis]] + spot[main_axis + 1:]
    return drawn.at[tuple(spot)].set(low).at[tuple(neighbour)].set(largest)


def steps_of(key, extent, cuts, smallest, high):
    def one(position, blocks):
        heights = jax.random.uniform(jax.random.fold_in(jax.random.fold_in(key, 6), position), (blocks,), jnp.float32, smallest / len(cuts), high / len(cuts))
        return jnp.repeat(jnp.exp(heights), extent[position] // blocks).reshape((-1,) + (1,) * (len(extent) - position - 1))

    factor_of = one(*cuts[0])
    for cut in cuts[1:]:
        factor_of = factor_of * one(*cut)
    return factor_of


def bell_draw(key, dims, spread, bound, pieces=(), kind=jnp.bfloat16):
    array = spread * jax.random.normal(key, dims, jnp.float32)
    if pieces:
        array = array * steps_of(key, dims, pieces, -0.22, 0.18)
    return jnp.clip(array, -bound, bound).astype(kind)


def setup_inputs(seed: int = 0) -> dict:
    keys = jax.random.split(jax.random.key(seed), 3)
    return {
        "traces": bell_draw(keys[0], (CHANNELS, MINUTES, NFFT), 1.0, 6.0, ((0, 64), (1, 4))),
        "live_flags": with_ends((jax.random.randint(keys[1], (CHANNELS,), 0, 8) < 7).astype(jnp.int32), jax.random.fold_in(keys[1], 1), 0, 1),
    }


def dft_table(fft_length):
    sample_index = jnp.arange(fft_length, dtype=jnp.float32)[:, None]
    bin_values = jnp.arange(fft_length // 2, dtype=jnp.float32)[None, :]
    hann_taper = 0.5 - 0.5 * jnp.cos(2.0 * jnp.pi * sample_index / fft_length)
    phase_angle = 2.0 * jnp.pi * jnp.mod(sample_index * bin_values, fft_length) / fft_length
    columns = jnp.concatenate([hann_taper * jnp.cos(phase_angle), -hann_taper * jnp.sin(phase_angle)], axis=1)
    return columns.astype(jnp.bfloat16)

def whiten_tile(traces_tile, flags_tile, smooth_half):
    channels_here, minutes_here, fft_length = traces_tile.shape
    half_length = fft_length // 2
    spectra = jnp.dot(traces_tile.reshape(channels_here * minutes_here, fft_length), dft_table(fft_length), preferred_element_type=jnp.float32)
    spec_real = spectra[:, :half_length]
    spec_imag = spectra[:, half_length:]
    power_sum = spec_real * spec_real + spec_imag * spec_imag
    bin_index = jnp.arange(half_length)
    band_matrix = (jnp.abs(bin_index[:, None] - bin_index[None, :]) <= smooth_half).astype(jnp.float32)
    bin_count = lax.optimization_barrier(jnp.sum(band_matrix, axis=0))
    smoothed = jnp.dot(power_sum, band_matrix, precision=lax.Precision.HIGHEST) / bin_count
    live_rows = jnp.repeat(flags_tile.astype(jnp.float32), minutes_here)[:, None]
    inverse_amp = live_rows * lax.rsqrt(smoothed + 1e-06)
    whitened = jnp.concatenate([spec_real * inverse_amp, spec_imag * inverse_amp], axis=1)
    return whitened.astype(jnp.bfloat16).reshape(channels_here, minutes_here, fft_length)

def lag_tables(fft_length, lag_count, bin_start, bin_width):
    bin_values = (bin_start + jnp.arange(bin_width)).astype(jnp.float32)[:, None]
    lag_index = (jnp.arange(lag_count) - lag_count // 2).astype(jnp.float32)[None, :]
    weight = jnp.where(bin_values == 0, 1.0, 2.0) / fft_length
    phase_angle = 2.0 * jnp.pi * jnp.mod(bin_values * lag_index, fft_length) / fft_length
    return (weight * jnp.cos(phase_angle), -weight * jnp.sin(phase_angle))

def skew_cut(cross_block, row_start, offs):
    bin_width, row_count, col_width = cross_block.shape
    flattened = cross_block.reshape(bin_width, row_count * col_width)
    flattened = jnp.pad(flattened, ((0, 0), (0, row_count)))
    skew_grid = flattened.reshape(bin_width, row_count, col_width + 1)
    return lax.dynamic_slice_in_dim(skew_grid, (row_start + 1).astype(jnp.int32), offs, axis=2)

def pair_lags(own_rows, tile_list, row_start, offs, lag_count):
    row_count = own_rows.shape[0]
    fft_length = own_rows.shape[2]
    half_length = fft_length // 2
    bin_width = min(128, half_length)
    lag_total = jnp.zeros((row_count, offs, lag_count), jnp.float32)
    for bin_start in range(0, half_length, bin_width):
        rows_real = own_rows[:, :, bin_start:bin_start + bin_width].astype(jnp.float32)
        rows_imag = own_rows[:, :, half_length + bin_start:half_length + bin_start + bin_width].astype(jnp.float32)
        parts_real = []
        parts_imag = []
        for neighbour_tile in tile_list:
            cols_real = neighbour_tile[:, :, bin_start:bin_start + bin_width].astype(jnp.float32)
            cols_imag = neighbour_tile[:, :, half_length + bin_start:half_length + bin_start + bin_width].astype(jnp.float32)
            real_real = jnp.einsum('cmk,jmk->kcj', rows_real, cols_real)
            imag_imag = jnp.einsum('cmk,jmk->kcj', rows_imag, cols_imag)
            imag_real = jnp.einsum('cmk,jmk->kcj', rows_imag, cols_real)
            real_imag = jnp.einsum('cmk,jmk->kcj', rows_real, cols_imag)
            parts_real.append(real_real + imag_imag)
            parts_imag.append(imag_real - real_imag)
        cross_real = skew_cut(jnp.concatenate(parts_real, axis=2), row_start, offs)
        cross_imag = skew_cut(jnp.concatenate(parts_imag, axis=2), row_start, offs)
        cos_table, sin_table = lag_tables(fft_length, lag_count, bin_start, bin_width)
        lag_total = lag_total + jnp.einsum('kco,kt->cot', cross_real, cos_table, precision=lax.Precision.HIGHEST)
        lag_total = lag_total + jnp.einsum('kco,kt->cot', cross_imag, sin_table, precision=lax.Precision.HIGHEST)
    return lag_total

def reference(traces, live_flags):
    tile_total = N_ROW * N_COL
    trace_tiles = traces.reshape(tile_total, CH_DEV, MINUTES, NFFT)
    flag_tiles = live_flags.reshape(tile_total, CH_DEV)

    def whiten_pair(both_parts):
        return whiten_tile(both_parts[0], both_parts[1], SMOOTH)
    whitened = lax.map(whiten_pair, (trace_tiles, flag_tiles)).reshape(CHANNELS, MINUTES, NFFT)
    padded = jnp.concatenate([whitened, jnp.zeros((OFFS, MINUTES, NFFT), jnp.bfloat16)], axis=0)

    def one_tile(tile_number):
        first_row = (tile_number * CH_DEV).astype(jnp.int32)
        own_rows = lax.dynamic_slice_in_dim(padded, first_row, CH_DEV, 0)
        window = lax.dynamic_slice_in_dim(padded, first_row, CH_DEV + OFFS, 0)
        lag_total = pair_lags(own_rows, [window], jnp.zeros((), jnp.int32), OFFS, LAGS)
        return lag_total.astype(jnp.bfloat16)
    stacked = lax.map(one_tile, jnp.arange(tile_total, dtype=jnp.int32))
    return stacked.reshape(CHANNELS, OFFS, LAGS)
```

```python
import jax
import jax.numpy as jnp
import numpy as np
from jax import lax
from jax.experimental import pallas as pl
from jax.experimental.pallas import tpu as pltpu
from jax.sharding import PartitionSpec as P

NFFT = 512
HALF = 256
OFFS = 256
LAGS = 256
SMOOTH = 32
AXES = ("row", "col", "tm")
LANES = 128
VMEM_BYTES = 48 * 1024 * 1024


def dft_table_t():
    n = np.arange(NFFT, dtype=np.float64)[None, :]
    k = np.arange(HALF, dtype=np.float64)[:, None]
    taper = 0.5 - 0.5 * np.cos(2.0 * np.pi * n / NFFT)
    phase = 2.0 * np.pi * np.mod(n * k, NFFT) / NFFT
    return np.concatenate([taper * np.cos(phase), -taper * np.sin(phase)], axis=0).astype(jnp.bfloat16)


def band_tables():
    k = np.arange(HALF)
    band = (np.abs(k[:, None] - k[None, :]) <= SMOOTH).astype(np.float32)
    inverse = np.broadcast_to(1.0 / band.sum(axis=1, keepdims=True), (HALF, LANES))
    return band.astype(jnp.bfloat16), inverse.astype(np.float32)


def lag_table():
    k = np.arange(HALF, dtype=np.float64)[:, None]
    t = (np.arange(LAGS) - LAGS // 2).astype(np.float64)[None, :]
    weight = np.where(k == 0, 1.0, 2.0) / NFFT
    phase = 2.0 * np.pi * np.mod(k * t, NFFT) / NFFT
    return np.concatenate([weight * np.cos(phase), -weight * np.sin(phase)], axis=0).astype(jnp.bfloat16)


def whiten_kernel(traces_ref, live_ref, table_ref, band_ref, inverse_ref, out_ref, scratch):
    table = table_ref[...]
    band = band_ref[...]
    inverse = inverse_ref[...]
    for pair in range(4):
        rows = jnp.concatenate(
            [traces_ref[high, 2 * pair + low] for low in range(2) for high in range(4)], axis=0
        )
        spectra = lax.dot_general(
            table, rows, (((1,), (1,)), ((), ())), preferred_element_type=jnp.float32
        )
        real, imag = spectra[:HALF], spectra[HALF:]
        power = real * real + imag * imag
        power_high = power.astype(jnp.bfloat16)
        power_low = (power - power_high.astype(jnp.float32)).astype(jnp.bfloat16)
        total = jnp.dot(band, power_high, preferred_element_type=jnp.float32) + jnp.dot(
            band, power_low, preferred_element_type=jnp.float32
        )
        for low in range(2):
            lanes = slice(low * LANES, (low + 1) * LANES)
            channel_low = 2 * pair + low
            smoothed = total[:, lanes] * inverse
            amplitude = live_ref[channel_low : channel_low + 1, :] * lax.rsqrt(smoothed + 1e-06)
            scratch[pl.ds(channel_low, HALF, stride=16), :] = real[:, lanes] * amplitude
            scratch[pl.ds(8 + channel_low, HALF, stride=16), :] = imag[:, lanes] * amplitude
    out_ref[...] = scratch[...].astype(jnp.bfloat16)


def cross_kernel(received_ref, flip_ref, out_ref, window):
    tiles = received_ref.shape[0]
    channels = tiles * 32
    lane_block = lax.broadcasted_iota(jnp.int32, (16, LANES), 1) // 32
    odd = lane_block % 2 == 1
    upper = lane_block >= 2
    window[pl.ds(channels, OFFS), :] = jnp.zeros((OFFS, 2 * LANES), jnp.bfloat16)

    def place(tile, carry):
        block = [received_ref[tile, source].astype(jnp.float32) for source in range(4)]
        step = []
        for first in (0, 2):
            step.append(jnp.where(odd, pltpu.roll(block[first + 1], 32, 1), block[first]))
            step.append(jnp.where(odd, block[first + 1], pltpu.roll(block[first], 96, 1)))
        by_high = [None] * 4
        for first in (0, 1):
            by_high[first] = jnp.where(upper, pltpu.roll(step[first + 2], 64, 1), step[first])
            by_high[first + 2] = jnp.where(upper, step[first + 2], pltpu.roll(step[first], 64, 1))
        for part in range(2):
            rows = jnp.concatenate([high[8 * part : 8 * part + 8] for high in by_high], axis=0)
            window[pl.ds(pl.multiple_of(tile * 32, 32), 32), part * LANES : (part + 1) * LANES] = (
                rows.astype(jnp.bfloat16)
            )
        return carry

    lax.fori_loop(0, tiles, place, 0, unroll=4)
    flip = flip_ref[...]

    def product(index, carry):
        start = pl.multiple_of(index * LANES, LANES)
        own = jnp.dot(flip, window[pl.ds(start, LANES), :], preferred_element_type=jnp.float32)
        real, imag = own[:, :LANES], own[:, LANES:]
        others = window[pl.ds(start, LANES + OFFS), :]
        for part, rows in enumerate(((real, imag), (imag, -real))):
            rows = jnp.concatenate(rows, axis=1).astype(jnp.bfloat16)
            cross = lax.dot_general(
                rows, others, (((1,), (1,)), ((), ())), preferred_element_type=jnp.float32
            )
            cross = pltpu.roll(cross, OFFS, 1, stride=1, stride_axis=0)
            for group in range(16):
                eight = cross[8 * group : 8 * group + 8]
                both = jnp.concatenate([eight[:, :LANES], eight[:, LANES : 2 * LANES]], axis=0)
                out_ref[index * 16 + 15 - group, part] = both.astype(jnp.bfloat16)
        return carry

    lax.fori_loop(0, channels // LANES, product, 0)


def lag_kernel(received_ref, table_ref, out_ref, scratch):
    scratch[...] = received_ref[...].astype(jnp.float32)
    table = table_ref[...]
    for channel in range(8):
        for upper in range(2):
            first = upper * 8 + 7 - channel
            real = scratch[pl.ds(first, HALF, stride=32), :]
            imag = scratch[pl.ds(16 + first, HALF, stride=32), :]
            both = jnp.concatenate([real, imag], axis=0).astype(jnp.bfloat16)
            lags = lax.dot_general(
                both, table, (((0,), (0,)), ((), ())), preferred_element_type=jnp.float32
            )
            out_ref[channel, upper * LANES : (upper + 1) * LANES, :] = lags.astype(jnp.bfloat16)


def call(kernel, shape, dtype, scratch):
    return pl.pallas_call(
        kernel,
        out_shape=jax.ShapeDtypeStruct(shape, dtype),
        scratch_shapes=[scratch],
        compiler_params=pltpu.CompilerParams(vmem_limit_bytes=VMEM_BYTES),
    )


def body(traces, live_flags):
    live = jnp.repeat(live_flags.astype(jnp.float32).reshape(4, 8).T, 32, axis=1)
    band, inverse = band_tables()
    whitened = call(
        whiten_kernel, (HALF * 16, LANES), jnp.bfloat16, pltpu.VMEM((HALF * 16, LANES), jnp.float32)
    )(traces.reshape(4, 8, 32, NFFT), live, jnp.asarray(dft_table_t()), jnp.asarray(band), jnp.asarray(inverse))
    one_bin = lax.all_to_all(whitened.reshape(HALF, 16, LANES), AXES, 0, 0, tiled=True)

    flip = np.eye(LANES, dtype=np.float32)[::-1].astype(jnp.bfloat16)
    cross = call(
        cross_kernel, (HALF, 2, 16, LANES), jnp.bfloat16, pltpu.VMEM((2048 + OFFS, 2 * LANES), jnp.bfloat16)
    )(one_bin.reshape(64, 4, 16, LANES), jnp.asarray(flip))
    all_bins = lax.all_to_all(cross.reshape(HALF, 32, LANES), AXES, 0, 0, tiled=True)

    return call(
        lag_kernel, (8, OFFS, LAGS), jnp.bfloat16, pltpu.VMEM((HALF * 32, LANES), jnp.float32)
    )(all_bins.reshape(HALF * 32, LANES), jnp.asarray(lag_table()))


def solution(mesh):
    return jax.shard_map(
        body,
        mesh=mesh,
        in_specs=(P(("row", "col"), "tm", None), P(("row", "col"))),
        out_specs=P(AXES, None, None),
        check_vma=False,
    )
```

```python
import jax
import jax.numpy as jnp
import numpy as np
from jax import lax
from jax.experimental import pallas as pl
from jax.experimental.pallas import tpu as pltpu
from jax.sharding import PartitionSpec as P

NFFT = 512
HALF = 256
OFFS = 256
LAGS = 256
SMOOTH = 32
CHANNELS = 2048
TILES = 64
AXES = ("row", "col", "tm")
LANES = 128
MIB = 1024 * 1024


def dft_table_t():
    n = np.arange(NFFT, dtype=np.float64)[None, :]
    k = np.arange(HALF, dtype=np.float64)[:, None]
    taper = 0.5 - 0.5 * np.cos(2.0 * np.pi * n / NFFT)
    phase = 2.0 * np.pi * np.mod(n * k, NFFT) / NFFT
    return np.concatenate([taper * np.cos(phase), -taper * np.sin(phase)], axis=0).astype(jnp.bfloat16)


def lag_table():
    k = np.arange(HALF, dtype=np.float64)[:, None]
    t = (np.arange(LAGS) - LAGS // 2).astype(np.float64)[None, :]
    weight = np.where(k == 0, 1.0, 2.0) / NFFT
    phase = 2.0 * np.pi * np.mod(k * t, NFFT) / NFFT
    return np.concatenate([weight * np.cos(phase), -weight * np.sin(phase)], axis=0).astype(jnp.bfloat16)


def zero_one(shape, holds):
    row = lax.broadcasted_iota(jnp.int32, shape, 0)
    column = lax.broadcasted_iota(jnp.int32, shape, 1)
    return jnp.where(holds(row, column), 1.0, 0.0).astype(jnp.bfloat16)


def product(left, right):
    return jnp.dot(left, right, preferred_element_type=jnp.float32)


def product_nt(left, right):
    return lax.dot_general(left, right, (((1,), (1,)), ((), ())), preferred_element_type=jnp.float32)


def whiten_kernel(flags_ref, traces_ref, table_ref, out_ref, scratch):
    band = zero_one((HALF, 2 * HALF), lambda r, c: jnp.abs(r - c % HALF) <= SMOOTH)
    bin_index = lax.broadcasted_iota(jnp.int32, (HALF, LANES), 0)
    count = jnp.minimum(bin_index + SMOOTH, HALF - 1) - jnp.maximum(bin_index - SMOOTH, 0) + 1
    inverse = 1.0 / count.astype(jnp.float32)
    lane_block = lax.broadcasted_iota(jnp.int32, (1, LANES), 1) // 32
    table = table_ref[...]
    width = 4
    for start in range(0, 8, width):
        rows = jnp.concatenate(
            [traces_ref[high, start + low] for low in range(width) for high in range(4)], axis=0
        )
        spectra = product_nt(table, rows)
        real, imag = spectra[:HALF], spectra[HALF:]
        power = real * real + imag * imag
        power_high = power.astype(jnp.bfloat16)
        power_low = (power - power_high.astype(jnp.float32)).astype(jnp.bfloat16)
        total = product(band, jnp.concatenate([power_high, power_low], axis=0))
        for low in range(width):
            lanes = slice(low * LANES, (low + 1) * LANES)
            channel_low = start + low
            live = jnp.zeros((1, LANES), jnp.float32)
            for high in range(4):
                live = jnp.where(lane_block == high, flags_ref[high * 8 + channel_low].astype(jnp.float32), live)
            amplitude = live * lax.rsqrt(total[:, lanes] * inverse + 1e-06)
            scratch[pl.ds(channel_low, HALF, stride=16), :] = real[:, lanes] * amplitude
            scratch[pl.ds(8 + channel_low, HALF, stride=16), :] = imag[:, lanes] * amplitude
    out_ref[...] = scratch[...].astype(jnp.bfloat16)


def cross_kernel(received_ref, out_ref, window):
    window[CHANNELS:, :] = jnp.zeros((OFFS, 2 * LANES), jnp.bfloat16)
    swap = zero_one(
        (4 * LANES, 4 * LANES),
        lambda r, c: (r % 32 == c % 32) & (r // 32 % 4 == c // 128) & (r // 128 == c // 32 % 4),
    )
    group = 16
    for first in range(0, TILES, group):
        side_by_side = jnp.concatenate(
            [received_ref[first : first + group, block].reshape(group * 16, LANES) for block in range(4)], axis=1
        )
        swapped = product(side_by_side, swap)
        for tile in range(group):
            for part in range(2):
                eight = swapped[tile * 16 + part * 8 : tile * 16 + part * 8 + 8]
                rows = jnp.concatenate([eight[:, high * LANES : (high + 1) * LANES] for high in range(4)], axis=0)
                start = (first + tile) * 32
                window[start : start + 32, part * LANES : (part + 1) * LANES] = rows.astype(jnp.bfloat16)

    flip = zero_one((LANES, LANES), lambda r, c: r + c == LANES - 1)

    def step(index, carry):
        start = pl.multiple_of(index * LANES, LANES)
        own = product(flip, window[pl.ds(start, LANES), :])
        real, imag = own[:, :LANES], own[:, LANES:]
        others = window[pl.ds(start, LANES + OFFS), :]
        rows = jnp.concatenate(
            [jnp.concatenate([real, imag], axis=1), jnp.concatenate([imag, -real], axis=1)], axis=0
        ).astype(jnp.bfloat16)
        both_parts = product_nt(rows, others)
        for part in range(2):
            cross = both_parts[part * LANES : (part + 1) * LANES]
            cross = pltpu.roll(cross, OFFS, 1, stride=1, stride_axis=0)
            for place in range(16):
                eight = cross[8 * place : 8 * place + 8]
                halves = jnp.concatenate([eight[:, :LANES], eight[:, LANES : 2 * LANES]], axis=0)
                out_ref[index * 16 + 15 - place, part] = halves.astype(jnp.bfloat16)
        return carry

    steps = CHANNELS // LANES
    lax.fori_loop(0, steps, step, 0, unroll=steps)


def lag_kernel(received_ref, table_ref, out_ref, lags, sems):
    table = table_ref[...]
    copies = []
    for channel in range(8):
        columns = []
        for upper in range(2):
            first = upper * 8 + 7 - channel
            real = received_ref[pl.ds(first, HALF, stride=32), :]
            imag = received_ref[pl.ds(16 + first, HALF, stride=32), :]
            columns.append(jnp.concatenate([real, imag], axis=0))
        both = jnp.concatenate(columns, axis=1)
        lags[channel] = lax.dot_general(
            both, table, (((0,), (0,)), ((), ())), preferred_element_type=jnp.float32
        ).astype(jnp.bfloat16)
        copy = pltpu.make_async_copy(lags.at[channel], out_ref.at[channel], sems.at[channel])
        copy.start()
        copies.append(copy)
    for copy in copies:
        copy.wait()


def call(kernel, shape, scratch, vmem_mib, **specs):
    return pl.pallas_call(
        kernel,
        out_shape=jax.ShapeDtypeStruct(shape, jnp.bfloat16),
        scratch_shapes=scratch,
        compiler_params=pltpu.CompilerParams(vmem_limit_bytes=vmem_mib * MIB),
        **specs,
    )


def body(traces, live_flags):
    vmem = pl.BlockSpec(memory_space=pltpu.VMEM)
    whitened = call(
        whiten_kernel,
        (HALF * 16, LANES),
        [pltpu.VMEM((HALF * 16, LANES), jnp.float32)],
        63,
        in_specs=[pl.BlockSpec(memory_space=pltpu.SMEM), vmem, vmem],
    )(live_flags, traces.reshape(4, 8, 32, NFFT), jnp.asarray(dft_table_t()))
    one_bin = lax.all_to_all(whitened.reshape(HALF, 16, LANES), AXES, 0, 0, tiled=True)

    cross = call(
        cross_kernel,
        (HALF, 2, 16, LANES),
        [pltpu.VMEM((CHANNELS + OFFS, 2 * LANES), jnp.bfloat16)],
        40,
    )(one_bin.reshape(TILES, 4, 16, LANES))
    all_bins = lax.all_to_all(cross.reshape(HALF, 32, LANES), AXES, 0, 0, tiled=True)

    return call(
        lag_kernel,
        (8, OFFS, LAGS),
        [pltpu.VMEM((8, OFFS, LAGS), jnp.bfloat16), pltpu.SemaphoreType.DMA((8,))],
        40,
        in_specs=[vmem, vmem],
        out_specs=pl.BlockSpec(memory_space=pltpu.HBM),
    )(all_bins.reshape(HALF * 32, LANES), jnp.asarray(lag_table()))


def solution(mesh):
    return jax.shard_map(
        body,
        mesh=mesh,
        in_specs=(P(("row", "col"), "tm", None), P(("row", "col"))),
        out_specs=P(AXES, None, None),
        check_vma=False,
    )
```

```python
import jax
import jax.numpy as jnp
import numpy as np
from jax import lax
from jax.experimental import pallas as pl
from jax.experimental.pallas import tpu as pltpu
from jax.sharding import PartitionSpec as P

NFFT = 512
HALF = 256
OFFS = 256
LAGS = 256
SMOOTH = 32
AXES = ("row", "col", "tm")
GROUP_AXES = ("col", "tm")
GROUP = 64
BINS = HALF // GROUP
ROW = 512
LANES = 128
MIB = 1024 * 1024


def dft_table_t():
    n = np.arange(NFFT, dtype=np.float64)[None, :]
    k = np.arange(HALF, dtype=np.float64)[:, None]
    taper = 0.5 - 0.5 * np.cos(2.0 * np.pi * n / NFFT)
    phase = 2.0 * np.pi * np.mod(n * k, NFFT) / NFFT
    return np.concatenate([taper * np.cos(phase), -taper * np.sin(phase)], axis=0).astype(jnp.bfloat16)


def lag_table():
    k = np.arange(HALF, dtype=np.float64)[:, None]
    t = (np.arange(LAGS) - LAGS // 2).astype(np.float64)[None, :]
    weight = np.where(k == 0, 1.0, 2.0) / NFFT
    phase = 2.0 * np.pi * np.mod(k * t, NFFT) / NFFT
    return np.concatenate([weight * np.cos(phase), -weight * np.sin(phase)], axis=0).astype(jnp.bfloat16)


def zero_one(shape, holds):
    row = lax.broadcasted_iota(jnp.int32, shape, 0)
    column = lax.broadcasted_iota(jnp.int32, shape, 1)
    return jnp.where(holds(row, column), 1.0, 0.0).astype(jnp.bfloat16)


def product(left, right):
    return jnp.dot(left, right, preferred_element_type=jnp.float32)


def product_nt(left, right):
    return lax.dot_general(left, right, (((1,), (1,)), ((), ())), preferred_element_type=jnp.float32)


def whiten_kernel(flags_ref, traces_ref, table_ref, out_ref, scratch, rounded, sems):
    band = zero_one((HALF, 2 * HALF), lambda r, c: jnp.abs(r - c % HALF) <= SMOOTH)
    bin_index = lax.broadcasted_iota(jnp.int32, (HALF, LANES), 0)
    count = jnp.minimum(bin_index + SMOOTH, HALF - 1) - jnp.maximum(bin_index - SMOOTH, 0) + 1
    inverse = 1.0 / count.astype(jnp.float32)
    lane_block = lax.broadcasted_iota(jnp.int32, (1, LANES), 1) // 32
    table = table_ref[...]
    width = 8
    for start in range(0, 8, width):
        rows = jnp.concatenate(
            [traces_ref[high, start + low] for low in range(width) for high in range(4)], axis=0
        )
        spectra = product_nt(table, rows)
        real, imag = spectra[:HALF], spectra[HALF:]
        power = real * real + imag * imag
        power_high = power.astype(jnp.bfloat16)
        power_low = (power - power_high.astype(jnp.float32)).astype(jnp.bfloat16)
        total = product(band, jnp.concatenate([power_high, power_low], axis=0))
        for low in range(width):
            lanes = slice(low * LANES, (low + 1) * LANES)
            channel_low = start + low
            live = jnp.zeros((1, LANES), jnp.float32)
            for high in range(4):
                live = jnp.where(lane_block == high, flags_ref[high * 8 + channel_low].astype(jnp.float32), live)
            amplitude = live * lax.rsqrt(total[:, lanes] * inverse + 1e-06)
            scratch[pl.ds(channel_low, HALF, stride=16), :] = real[:, lanes] * amplitude
            scratch[pl.ds(8 + channel_low, HALF, stride=16), :] = imag[:, lanes] * amplitude
    copies = []
    rows = HALF * 4
    for piece in range(4):
        part = pl.ds(piece * rows, rows)
        rounded[part, :] = scratch[part, :].astype(jnp.bfloat16)
        copies.append(pltpu.make_async_copy(rounded.at[part], out_ref.at[part], sems.at[piece]))
        copies[-1].start()
    for copy in copies:
        copy.wait()


def swap_table():
    r = np.arange(4 * LANES)[:, None]
    c = np.arange(4 * LANES)[None, :]
    same = (r % 32 == c % 32) & (r // 32 % 4 == c // 128) & (r // 128 == c // 32 % 4)
    return same.astype(np.float32).astype(jnp.bfloat16)


def flip_table():
    return np.eye(LANES, dtype=np.float32)[::-1].astype(jnp.bfloat16)


def place_tiles(received_ref, swap, index, window, first_row):
    tiles = received_ref.shape[0]
    side_by_side = jnp.concatenate(
        [received_ref[:, block, index].reshape(tiles * 16, LANES) for block in range(4)], axis=1
    )
    swapped = product(side_by_side, swap)
    for tile in range(tiles):
        for part in range(2):
            eight = swapped[tile * 16 + part * 8 : tile * 16 + part * 8 + 8]
            rows = jnp.concatenate([eight[:, high * LANES : (high + 1) * LANES] for high in range(4)], axis=0)
            start = first_row + tile * 32
            window[index, start : start + 32, part * LANES : (part + 1) * LANES] = rows.astype(jnp.bfloat16)


def cross_block(window, index, start, flip, out_ref, first_place):
    own = product(flip, window[index, start : start + LANES, :])
    real, imag = own[:, :LANES], own[:, LANES:]
    others = window[index, start : start + LANES + OFFS, :]
    rows = jnp.concatenate(
        [jnp.concatenate([real, imag], axis=1), jnp.concatenate([imag, -real], axis=1)], axis=0
    ).astype(jnp.bfloat16)
    both_parts = product_nt(rows, others)
    for part in range(2):
        cross = both_parts[part * LANES : (part + 1) * LANES]
        cross = pltpu.roll(cross, OFFS, 1, stride=1, stride_axis=0)
        for place in range(16):
            eight = cross[8 * place : 8 * place + 8]
            halves = jnp.concatenate([eight[:, :LANES], eight[:, LANES : 2 * LANES]], axis=0)
            out_ref[first_place + 15 - place, index, part] = halves.astype(jnp.bfloat16)


def near_kernel(received_ref, swap_ref, flip_ref, out_ref, rest_ref, window):
    swap = swap_ref[...]
    flip = flip_ref[...]
    half = window.shape[1] // 2
    for index in range(BINS):
        place_tiles(received_ref, swap, index, window, 0)
        rest_ref[index] = window[index, half:]
        for start in range(0, half, LANES):
            cross_block(window, index, start, flip, out_ref, start // 8)


def far_kernel(halo_ref, rest_ref, swap_ref, flip_ref, cross_ref, out_ref, window, results, sems):
    del cross_ref
    swap = swap_ref[...]
    flip = flip_ref[...]
    half = rest_ref.shape[1]
    places = half // 8
    copies = []
    for index in range(BINS):
        window[index, :half] = rest_ref[index]
        place_tiles(halo_ref, swap, index, window, half)
        for start in range(0, half, LANES):
            cross_block(window, index, start, flip, results, start // 8)
        copies.append(
            pltpu.make_async_copy(results.at[:, index], out_ref.at[pl.ds(places, places), index], sems.at[index])
        )
        copies[-1].start()
    for copy in copies:
        copy.wait()


def lag_kernel(received_ref, table_ref, out_ref, lags, sems):
    table = table_ref[...]
    copies = []
    for channel in range(8):
        columns = []
        for upper in range(2):
            first = upper * 8 + 7 - channel
            real = received_ref[pl.ds(first, HALF, stride=32), :]
            imag = received_ref[pl.ds(16 + first, HALF, stride=32), :]
            columns.append(jnp.concatenate([real, imag], axis=0))
        both = jnp.concatenate(columns, axis=1)
        lags[channel] = lax.dot_general(
            both, table, (((0,), (0,)), ((), ())), preferred_element_type=jnp.float32
        ).astype(jnp.bfloat16)
        if channel % 2:
            pair = pl.ds(channel - 1, 2)
            copies.append(pltpu.make_async_copy(lags.at[pair], out_ref.at[pair], sems.at[channel // 2]))
            copies[-1].start()
    for copy in copies:
        copy.wait()


def call(kernel, shape, scratch, vmem_mib, **options):
    return pl.pallas_call(
        kernel,
        out_shape=jax.tree.map(lambda s: jax.ShapeDtypeStruct(s, jnp.bfloat16), shape, is_leaf=lambda s: isinstance(s, tuple)),
        scratch_shapes=scratch,
        compiler_params=pltpu.CompilerParams(vmem_limit_bytes=vmem_mib * MIB),
        **options,
    )


def body(traces, live_flags):
    vmem = pl.BlockSpec(memory_space=pltpu.VMEM)
    hbm = pl.BlockSpec(memory_space=pltpu.HBM)
    anywhere = pl.BlockSpec(memory_space=pl.ANY)
    whitened = call(
        whiten_kernel,
        (HALF * 16, LANES),
        [
            pltpu.VMEM((HALF * 16, LANES), jnp.float32),
            pltpu.VMEM((HALF * 16, LANES), jnp.bfloat16),
            pltpu.SemaphoreType.DMA((4,)),
        ],
        63,
        in_specs=[pl.BlockSpec(memory_space=pltpu.SMEM), vmem, vmem],
        out_specs=hbm,
    )(live_flags, traces.reshape(4, 8, 32, NFFT), jnp.asarray(dft_table_t()))
    some_bins = lax.all_to_all(whitened.reshape(GROUP, BINS, 16, LANES), GROUP_AXES, 0, 0, tiled=True)
    some_bins = some_bins.reshape(ROW // 32, 4, BINS, 16, LANES)

    first = some_bins[: OFFS // 32]
    halo = lax.ppermute(first, "row", [(1, 0), (2, 1), (3, 2)])
    swap, flip = jnp.asarray(swap_table()), jnp.asarray(flip_table())
    cross, rest = call(
        near_kernel,
        [(GROUP, BINS, 2, 16, LANES), (BINS, ROW // 2, 2 * LANES)],
        [pltpu.VMEM((BINS, ROW, 2 * LANES), jnp.bfloat16)],
        32,
    )(some_bins, swap, flip)
    cross = call(
        far_kernel,
        (GROUP, BINS, 2, 16, LANES),
        [
            pltpu.VMEM((BINS, ROW // 2 + OFFS, 2 * LANES), jnp.bfloat16),
            pltpu.VMEM((GROUP // 2, BINS, 2, 16, LANES), jnp.bfloat16),
            pltpu.SemaphoreType.DMA((BINS,)),
        ],
        32,
        in_specs=[vmem, vmem, vmem, vmem, anywhere],
        out_specs=anywhere,
        input_output_aliases={4: 0},
    )(halo, rest, swap, flip, cross)
    all_bins = lax.all_to_all(cross.reshape(GROUP, BINS * 32, LANES), GROUP_AXES, 0, 0, tiled=True)

    return call(
        lag_kernel,
        (8, OFFS, LAGS),
        [pltpu.VMEM((8, OFFS, LAGS), jnp.bfloat16), pltpu.SemaphoreType.DMA((4,))],
        32,
        in_specs=[vmem, vmem],
        out_specs=hbm,
    )(all_bins.reshape(HALF * 32, LANES), jnp.asarray(lag_table()))


def solution(mesh):
    return jax.shard_map(
        body,
        mesh=mesh,
        in_specs=(P(("row", "col"), "tm", None), P(("row", "col"))),
        out_specs=P(AXES, None, None),
        check_vma=False,
    )
```

```python
import jax
import jax.numpy as jnp
import numpy as np
from jax import lax
from jax.experimental import pallas as pl
from jax.experimental.pallas import tpu as pltpu
from jax.sharding import PartitionSpec as P

NFFT = 512
HALF = 256
OFFS = 256
LAGS = 256
SMOOTH = 32
CHANNELS = 2048
TILES = 64
AXES = ("row", "col", "tm")
LANES = 128
MIB = 1024 * 1024


def dft_table_t():
    n = np.arange(NFFT, dtype=np.float64)[None, :]
    k = np.arange(HALF, dtype=np.float64)[:, None]
    taper = 0.5 - 0.5 * np.cos(2.0 * np.pi * n / NFFT)
    phase = 2.0 * np.pi * np.mod(n * k, NFFT) / NFFT
    return np.concatenate([taper * np.cos(phase), -taper * np.sin(phase)], axis=0).astype(jnp.bfloat16)


def lag_table():
    k = np.arange(HALF, dtype=np.float64)[:, None]
    t = (np.arange(LAGS) - LAGS // 2).astype(np.float64)[None, :]
    weight = np.where(k == 0, 1.0, 2.0) / NFFT
    phase = 2.0 * np.pi * np.mod(k * t, NFFT) / NFFT
    return np.concatenate([weight * np.cos(phase), -weight * np.sin(phase)], axis=0).astype(jnp.bfloat16)


def zero_one(shape, holds):
    row = lax.broadcasted_iota(jnp.int32, shape, 0)
    column = lax.broadcasted_iota(jnp.int32, shape, 1)
    return jnp.where(holds(row, column), 1.0, 0.0).astype(jnp.bfloat16)


def product(left, right):
    return jnp.dot(left, right, preferred_element_type=jnp.float32)


def product_nt(left, right):
    return lax.dot_general(left, right, (((1,), (1,)), ((), ())), preferred_element_type=jnp.float32)


def whiten_kernel(flags_ref, traces_ref, table_ref, out_ref, scratch, rounded, sems):
    band = zero_one((HALF, 2 * HALF), lambda r, c: jnp.abs(r - c % HALF) <= SMOOTH)
    bin_index = lax.broadcasted_iota(jnp.int32, (HALF, LANES), 0)
    count = jnp.minimum(bin_index + SMOOTH, HALF - 1) - jnp.maximum(bin_index - SMOOTH, 0) + 1
    inverse = 1.0 / count.astype(jnp.float32)
    lane_block = lax.broadcasted_iota(jnp.int32, (1, LANES), 1) // 32
    table = table_ref[...]
    width = 8
    for start in range(0, 8, width):
        rows = jnp.concatenate(
            [traces_ref[high, start + low] for low in range(width) for high in range(4)], axis=0
        )
        spectra = product_nt(table, rows)
        real, imag = spectra[:HALF], spectra[HALF:]
        power = real * real + imag * imag
        power_high = power.astype(jnp.bfloat16)
        power_low = (power - power_high.astype(jnp.float32)).astype(jnp.bfloat16)
        total = product(band, jnp.concatenate([power_high, power_low], axis=0))
        for low in range(width):
            lanes = slice(low * LANES, (low + 1) * LANES)
            channel_low = start + low
            live = jnp.zeros((1, LANES), jnp.float32)
            for high in range(4):
                live = jnp.where(lane_block == high, flags_ref[high * 8 + channel_low].astype(jnp.float32), live)
            amplitude = live * lax.rsqrt(total[:, lanes] * inverse + 1e-06)
            scratch[pl.ds(channel_low, HALF, stride=16), :] = real[:, lanes] * amplitude
            scratch[pl.ds(8 + channel_low, HALF, stride=16), :] = imag[:, lanes] * amplitude
    copies = []
    rows = HALF * 4
    for piece in range(4):
        part = pl.ds(piece * rows, rows)
        rounded[part, :] = scratch[part, :].astype(jnp.bfloat16)
        copies.append(pltpu.make_async_copy(rounded.at[part], out_ref.at[part], sems.at[piece]))
        copies[-1].start()
    for copy in copies:
        copy.wait()


def swap_table():
    r = np.arange(4 * LANES)[:, None]
    c = np.arange(4 * LANES)[None, :]
    same = (r % 32 == c % 32) & (r // 32 % 4 == c // 128) & (r // 128 == c // 32 % 4)
    return same.astype(np.float32).astype(jnp.bfloat16)


def flip_table():
    return np.eye(LANES, dtype=np.float32)[::-1].astype(jnp.bfloat16)


def cross_kernel(received_ref, swap_ref, flip_ref, out_ref, window, own):
    window[CHANNELS:, :] = jnp.zeros((OFFS, 2 * LANES), jnp.bfloat16)
    swap = swap_ref[...]
    group = 16
    for first in range(0, TILES, group):
        side_by_side = jnp.concatenate(
            [received_ref[first : first + group, block].reshape(group * 16, LANES) for block in range(4)], axis=1
        )
        swapped = product(side_by_side, swap)
        for tile in range(group):
            for part in range(2):
                eight = swapped[tile * 16 + part * 8 : tile * 16 + part * 8 + 8]
                rows = jnp.concatenate([eight[:, high * LANES : (high + 1) * LANES] for high in range(4)], axis=0)
                start = (first + tile) * 32
                window[start : start + 32, part * LANES : (part + 1) * LANES] = rows.astype(jnp.bfloat16)

    flip = flip_ref[...]
    for block in range(CHANNELS // LANES):
        turned = product(flip, window[block * LANES : (block + 1) * LANES, :])
        real, imag = turned[:, :LANES], turned[:, LANES:]
        own[block, :LANES] = jnp.concatenate([real, imag], axis=1).astype(jnp.bfloat16)
        own[block, LANES:] = jnp.concatenate([imag, -real], axis=1).astype(jnp.bfloat16)

    for block in range(CHANNELS // LANES):
        start = block * LANES
        both_parts = product_nt(own[block], window[start : start + LANES + OFFS, :])
        for part in range(2):
            cross = both_parts[part * LANES : (part + 1) * LANES]
            cross = pltpu.roll(cross, OFFS, 1, stride=1, stride_axis=0)
            for place in range(16):
                eight = cross[8 * place : 8 * place + 8]
                halves = jnp.concatenate([eight[:, :LANES], eight[:, LANES : 2 * LANES]], axis=0)
                out_ref[block * 16 + 15 - place, part] = halves.astype(jnp.bfloat16)


def lag_kernel(received_ref, table_ref, out_ref, lags, sems):
    table = table_ref[...]
    copies = []
    for channel in range(8):
        columns = []
        for upper in range(2):
            first = upper * 8 + 7 - channel
            real = received_ref[pl.ds(first, HALF, stride=32), :]
            imag = received_ref[pl.ds(16 + first, HALF, stride=32), :]
            columns.append(jnp.concatenate([real, imag], axis=0))
        both = jnp.concatenate(columns, axis=1)
        lags[channel] = lax.dot_general(
            both, table, (((0,), (0,)), ((), ())), preferred_element_type=jnp.float32
        ).astype(jnp.bfloat16)
        if channel % 2:
            pair = pl.ds(channel - 1, 2)
            copies.append(pltpu.make_async_copy(lags.at[pair], out_ref.at[pair], sems.at[channel // 2]))
            copies[-1].start()
    for copy in copies:
        copy.wait()


def call(kernel, shape, scratch, vmem_mib, **specs):
    return pl.pallas_call(
        kernel,
        out_shape=jax.ShapeDtypeStruct(shape, jnp.bfloat16),
        scratch_shapes=scratch,
        compiler_params=pltpu.CompilerParams(vmem_limit_bytes=vmem_mib * MIB),
        **specs,
    )


def body(traces, live_flags):
    vmem = pl.BlockSpec(memory_space=pltpu.VMEM)
    whitened = call(
        whiten_kernel,
        (HALF * 16, LANES),
        [
            pltpu.VMEM((HALF * 16, LANES), jnp.float32),
            pltpu.VMEM((HALF * 16, LANES), jnp.bfloat16),
            pltpu.SemaphoreType.DMA((4,)),
        ],
        63,
        in_specs=[pl.BlockSpec(memory_space=pltpu.SMEM), vmem, vmem],
        out_specs=pl.BlockSpec(memory_space=pltpu.HBM),
    )(live_flags, traces.reshape(4, 8, 32, NFFT), jnp.asarray(dft_table_t()))
    one_bin = lax.all_to_all(whitened.reshape(HALF, 16, LANES), AXES, 0, 0, tiled=True)

    cross = call(
        cross_kernel,
        (HALF, 2, 16, LANES),
        [
            pltpu.VMEM((CHANNELS + OFFS, 2 * LANES), jnp.bfloat16),
            pltpu.VMEM((CHANNELS // LANES, 2 * LANES, 2 * LANES), jnp.bfloat16),
        ],
        40,
    )(one_bin.reshape(TILES, 4, 16, LANES), jnp.asarray(swap_table()), jnp.asarray(flip_table()))
    all_bins = lax.all_to_all(cross.reshape(HALF, 32, LANES), AXES, 0, 0, tiled=True)

    return call(
        lag_kernel,
        (8, OFFS, LAGS),
        [pltpu.VMEM((8, OFFS, LAGS), jnp.bfloat16), pltpu.SemaphoreType.DMA((4,))],
        40,
        in_specs=[vmem, vmem],
        out_specs=pl.BlockSpec(memory_space=pltpu.HBM),
    )(all_bins.reshape(HALF * 32, LANES), jnp.asarray(lag_table()))


def solution(mesh):
    return jax.shard_map(
        body,
        mesh=mesh,
        in_specs=(P(("row", "col"), "tm", None), P(("row", "col"))),
        out_specs=P(AXES, None, None),
        check_vma=False,
    )
```

```python
import jax
import jax.numpy as jnp
import numpy as np
from jax import lax
from jax.experimental import pallas as pl
from jax.experimental.pallas import tpu as pltpu
from jax.sharding import PartitionSpec as P

NFFT = 512
LANES = 128
HALF = 256
OFFS = 256
LAGS = 256
SMOOTH = 32
AXES = ("row", "col", "tm")
GROUP_AXES = ("col", "tm")
GROUP = 64
BINS = HALF // GROUP
ROW = 512
HALF_BLOCKS = ROW // 2 // LANES
MIB = 1024 * 1024


def dft_table_t():
    n = np.arange(NFFT, dtype=np.float64)[None, :]
    k = np.arange(HALF, dtype=np.float64)[:, None]
    taper = 0.5 - 0.5 * np.cos(2.0 * np.pi * n / NFFT)
    phase = 2.0 * np.pi * np.mod(n * k, NFFT) / NFFT
    return np.concatenate([taper * np.cos(phase), -taper * np.sin(phase)], axis=0).astype(jnp.bfloat16)


def lag_table():
    k = np.arange(HALF, dtype=np.float64)[:, None]
    t = (np.arange(LAGS) - LAGS // 2).astype(np.float64)[None, :]
    weight = np.where(k == 0, 1.0, 2.0) / NFFT
    phase = 2.0 * np.pi * np.mod(k * t, NFFT) / NFFT
    return np.concatenate([weight * np.cos(phase), -weight * np.sin(phase)], axis=0).astype(jnp.bfloat16)


def zero_one(shape, holds):
    row = lax.broadcasted_iota(jnp.int32, shape, 0)
    column = lax.broadcasted_iota(jnp.int32, shape, 1)
    return jnp.where(holds(row, column), 1.0, 0.0).astype(jnp.bfloat16)


def product(left, right):
    return jnp.dot(left, right, preferred_element_type=jnp.float32)


def product_nt(left, right):
    return lax.dot_general(left, right, (((1,), (1,)), ((), ())), preferred_element_type=jnp.float32)


def whiten_kernel(flags_ref, traces_ref, table_ref, out_ref, scratch, rounded, sems):
    band = zero_one((HALF, 2 * HALF), lambda r, c: jnp.abs(r - c % HALF) <= SMOOTH)
    bin_index = lax.broadcasted_iota(jnp.int32, (HALF, LANES), 0)
    count = jnp.minimum(bin_index + SMOOTH, HALF - 1) - jnp.maximum(bin_index - SMOOTH, 0) + 1
    inverse = 1.0 / count.astype(jnp.float32)
    lane_block = lax.broadcasted_iota(jnp.int32, (1, LANES), 1) // 32
    table = table_ref[...]
    width = 8
    for start in range(0, 8, width):
        rows = jnp.concatenate(
            [traces_ref[high, start + low] for low in range(width) for high in range(4)], axis=0
        )
        spectra = product_nt(table, rows)
        real, imag = spectra[:HALF], spectra[HALF:]
        power = real * real + imag * imag
        power_high = power.astype(jnp.bfloat16)
        power_low = (power - power_high.astype(jnp.float32)).astype(jnp.bfloat16)
        total = product(band, jnp.concatenate([power_high, power_low], axis=0))
        for low in range(width):
            lanes = slice(low * LANES, (low + 1) * LANES)
            channel_low = start + low
            live = jnp.zeros((1, LANES), jnp.float32)
            for high in range(4):
                live = jnp.where(lane_block == high, flags_ref[high * 8 + channel_low].astype(jnp.float32), live)
            amplitude = live * lax.rsqrt(total[:, lanes] * inverse + 1e-06)
            scratch[pl.ds(channel_low, HALF, stride=16), :] = real[:, lanes] * amplitude
            scratch[pl.ds(8 + channel_low, HALF, stride=16), :] = imag[:, lanes] * amplitude
    copies = []
    rows = HALF * 4
    for piece in range(4):
        part = pl.ds(piece * rows, rows)
        rounded[part, :] = scratch[part, :].astype(jnp.bfloat16)
        copies.append(pltpu.make_async_copy(rounded.at[part], out_ref.at[part], sems.at[piece]))
        copies[-1].start()
    for copy in copies:
        copy.wait()


def swap_table():
    r = np.arange(4 * LANES)[:, None]
    c = np.arange(4 * LANES)[None, :]
    same = (r % 32 == c % 32) & (r // 32 % 4 == c // 128) & (r // 128 == c // 32 % 4)
    return same.astype(np.float32).astype(jnp.bfloat16)


def flip_table():
    return np.eye(LANES, dtype=np.float32)[::-1].astype(jnp.bfloat16)


def place_tiles(received_ref, swap, index, window, first_row):
    tiles = received_ref.shape[0]
    side_by_side = jnp.concatenate(
        [received_ref[:, block, index].reshape(tiles * 16, LANES) for block in range(4)], axis=1
    )
    swapped = product(side_by_side, swap)
    for tile in range(tiles):
        for part in range(2):
            eight = swapped[tile * 16 + part * 8 : tile * 16 + part * 8 + 8]
            rows = jnp.concatenate([eight[:, high * LANES : (high + 1) * LANES] for high in range(4)], axis=0)
            start = first_row + tile * 32
            window[index, start : start + 32, part * LANES : (part + 1) * LANES] = rows.astype(jnp.bfloat16)


def turn_blocks(window, flip, index, own):
    for block in range(own.shape[1]):
        turned = product(flip, window[index, block * LANES : (block + 1) * LANES, :])
        real, imag = turned[:, :LANES], turned[:, LANES:]
        own[index, block, :LANES] = jnp.concatenate([real, imag], axis=1).astype(jnp.bfloat16)
        own[index, block, LANES:] = jnp.concatenate([imag, -real], axis=1).astype(jnp.bfloat16)


def cross_block(own, others, index, block, out_ref):
    both_parts = product_nt(own, others)
    for part in range(2):
        cross = both_parts[part * LANES : (part + 1) * LANES]
        cross = pltpu.roll(cross, OFFS, 1, stride=1, stride_axis=0)
        for place in range(16):
            eight = cross[8 * place : 8 * place + 8]
            halves = jnp.concatenate([eight[:, :LANES], eight[:, LANES : 2 * LANES]], axis=0)
            out_ref[block * 16 + 15 - place, index, part] = halves.astype(jnp.bfloat16)


def near_kernel(received_ref, swap_ref, flip_ref, out_ref, window, own):
    swap = swap_ref[...]
    flip = flip_ref[...]
    for index in range(BINS):
        place_tiles(received_ref, swap, index, window, 0)
    for index in range(BINS):
        turn_blocks(window, flip, index, own)
    for index in range(BINS):
        for block in range(HALF_BLOCKS):
            start = block * LANES
            cross_block(own[index, block], window[index, start : start + LANES + OFFS], index, block, out_ref)


def far_kernel(halo_ref, window_ref, own_ref, swap_ref, cross_ref, out_ref, beyond, results, sems):
    del cross_ref
    swap = swap_ref[...]
    places = ROW // 2 // 8
    for index in range(BINS):
        place_tiles(halo_ref, swap, index, beyond, 0)
    copies = []
    for index in range(BINS):
        for block in range(HALF_BLOCKS):
            start = block * LANES
            others = jnp.concatenate(
                [window_ref[index, ROW // 2 + start :], beyond[index, : start + LANES]], axis=0
            )
            cross_block(own_ref[index, HALF_BLOCKS + block], others, index, block, results)
        copies.append(
            pltpu.make_async_copy(results.at[:, index], out_ref.at[pl.ds(places, places), index], sems.at[index])
        )
        copies[-1].start()
    for copy in copies:
        copy.wait()


def lag_kernel(received_ref, table_ref, out_ref, lags, sems):
    table = table_ref[...]
    copies = []
    for channel in range(8):
        columns = []
        for upper in range(2):
            first = upper * 8 + 7 - channel
            real = received_ref[pl.ds(first, HALF, stride=32), :]
            imag = received_ref[pl.ds(16 + first, HALF, stride=32), :]
            columns.append(jnp.concatenate([real, imag], axis=0))
        both = jnp.concatenate(columns, axis=1)
        lags[channel] = lax.dot_general(
            both, table, (((0,), (0,)), ((), ())), preferred_element_type=jnp.float32
        ).astype(jnp.bfloat16)
        if channel % 2:
            pair = pl.ds(channel - 1, 2)
            copies.append(pltpu.make_async_copy(lags.at[pair], out_ref.at[pair], sems.at[channel // 2]))
            copies[-1].start()
    for copy in copies:
        copy.wait()


def call(kernel, shape, scratch, vmem_mib, **options):
    return pl.pallas_call(
        kernel,
        out_shape=jax.tree.map(lambda s: jax.ShapeDtypeStruct(s, jnp.bfloat16), shape, is_leaf=lambda s: isinstance(s, tuple)),
        scratch_shapes=scratch,
        compiler_params=pltpu.CompilerParams(vmem_limit_bytes=vmem_mib * MIB),
        **options,
    )


def body(traces, live_flags):
    vmem = pl.BlockSpec(memory_space=pltpu.VMEM)
    hbm = pl.BlockSpec(memory_space=pltpu.HBM)
    anywhere = pl.BlockSpec(memory_space=pl.ANY)
    whitened = call(
        whiten_kernel,
        (HALF * 16, LANES),
        [
            pltpu.VMEM((HALF * 16, LANES), jnp.float32),
            pltpu.VMEM((HALF * 16, LANES), jnp.bfloat16),
            pltpu.SemaphoreType.DMA((4,)),
        ],
        63,
        in_specs=[pl.BlockSpec(memory_space=pltpu.SMEM), vmem, vmem],
        out_specs=hbm,
    )(live_flags, traces.reshape(4, 8, 32, NFFT), jnp.asarray(dft_table_t()))
    some_bins = lax.all_to_all(whitened.reshape(GROUP, BINS, 16, LANES), GROUP_AXES, 0, 0, tiled=True)
    some_bins = some_bins.reshape(ROW // 32, 4, BINS, 16, LANES)

    first = some_bins[: OFFS // 32]
    halo = lax.ppermute(first, "row", [(1, 0), (2, 1), (3, 2)])
    swap, flip = jnp.asarray(swap_table()), jnp.asarray(flip_table())
    cross, window, own = call(
        near_kernel,
        [
            (GROUP, BINS, 2, 16, LANES),
            (BINS, ROW, 2 * LANES),
            (BINS, 2 * HALF_BLOCKS, 2 * LANES, 2 * LANES),
        ],
        [],
        32,
    )(some_bins, swap, flip)
    cross = call(
        far_kernel,
        (GROUP, BINS, 2, 16, LANES),
        [
            pltpu.VMEM((BINS, OFFS, 2 * LANES), jnp.bfloat16),
            pltpu.VMEM((GROUP // 2, BINS, 2, 16, LANES), jnp.bfloat16),
            pltpu.SemaphoreType.DMA((BINS,)),
        ],
        32,
        in_specs=[vmem, vmem, vmem, vmem, anywhere],
        out_specs=anywhere,
        input_output_aliases={4: 0},
    )(halo, window, own, swap, cross)
    all_bins = lax.all_to_all(cross.reshape(GROUP, BINS * 32, LANES), GROUP_AXES, 0, 0, tiled=True)

    return call(
        lag_kernel,
        (8, OFFS, LAGS),
        [pltpu.VMEM((8, OFFS, LAGS), jnp.bfloat16), pltpu.SemaphoreType.DMA((4,))],
        32,
        in_specs=[vmem, vmem],
        out_specs=hbm,
    )(all_bins.reshape(HALF * 32, LANES), jnp.asarray(lag_table()))


def solution(mesh):
    return jax.shard_map(
        body,
        mesh=mesh,
        in_specs=(P(("row", "col"), "tm", None), P(("row", "col"))),
        out_specs=P(AXES, None, None),
        check_vma=False,
    )
```

```python
import jax
import jax.numpy as jnp
import numpy as np
from jax import lax
from jax.experimental import pallas as pl
from jax.experimental.pallas import tpu as pltpu
from jax.sharding import PartitionSpec as P

NFFT = 512
HALF = 256
OFFS = 256
LAGS = 256
SMOOTH = 32
CHANNELS = 2048
TILES = 64
AXES = ("row", "col", "tm")
LANES = 128
MIB = 1024 * 1024


def dft_table_t():
    n = np.arange(NFFT, dtype=np.float64)[None, :]
    k = np.arange(HALF, dtype=np.float64)[:, None]
    taper = 0.5 - 0.5 * np.cos(2.0 * np.pi * n / NFFT)
    phase = 2.0 * np.pi * np.mod(n * k, NFFT) / NFFT
    return np.concatenate([taper * np.cos(phase), -taper * np.sin(phase)], axis=0).astype(jnp.bfloat16)


def lag_table():
    k = np.arange(HALF, dtype=np.float64)[:, None]
    t = (np.arange(LAGS) - LAGS // 2).astype(np.float64)[None, :]
    weight = np.where(k == 0, 1.0, 2.0) / NFFT
    phase = 2.0 * np.pi * np.mod(k * t, NFFT) / NFFT
    return np.concatenate([weight * np.cos(phase), -weight * np.sin(phase)], axis=0).astype(jnp.bfloat16)


def zero_one(shape, holds):
    row = lax.broadcasted_iota(jnp.int32, shape, 0)
    column = lax.broadcasted_iota(jnp.int32, shape, 1)
    return jnp.where(holds(row, column), 1.0, 0.0).astype(jnp.bfloat16)


def product(left, right):
    return jnp.dot(left, right, preferred_element_type=jnp.float32)


def product_nt(left, right):
    return lax.dot_general(left, right, (((1,), (1,)), ((), ())), preferred_element_type=jnp.float32)


def whiten_kernel(flags_ref, traces_ref, table_ref, out_ref, scratch, rounded, sems):
    band = zero_one((HALF, 2 * HALF), lambda r, c: jnp.abs(r - c % HALF) <= SMOOTH)
    bin_index = lax.broadcasted_iota(jnp.int32, (HALF, LANES), 0)
    count = jnp.minimum(bin_index + SMOOTH, HALF - 1) - jnp.maximum(bin_index - SMOOTH, 0) + 1
    inverse = 1.0 / count.astype(jnp.float32)
    lane_block = lax.broadcasted_iota(jnp.int32, (1, LANES), 1) // 32
    table = table_ref[...]
    width = 8
    for start in range(0, 8, width):
        rows = jnp.concatenate(
            [traces_ref[high, start + low] for low in range(width) for high in range(4)], axis=0
        )
        spectra = product_nt(table, rows)
        real, imag = spectra[:HALF], spectra[HALF:]
        power = real * real + imag * imag
        power_high = power.astype(jnp.bfloat16)
        power_low = (power - power_high.astype(jnp.float32)).astype(jnp.bfloat16)
        total = product(band, jnp.concatenate([power_high, power_low], axis=0))
        for low in range(width):
            lanes = slice(low * LANES, (low + 1) * LANES)
            channel_low = start + low
            live = jnp.zeros((1, LANES), jnp.float32)
            for high in range(4):
                live = jnp.where(lane_block == high, flags_ref[high * 8 + channel_low].astype(jnp.float32), live)
            amplitude = live * lax.rsqrt(total[:, lanes] * inverse + 1e-06)
            scratch[pl.ds(channel_low, HALF, stride=16), :] = real[:, lanes] * amplitude
            scratch[pl.ds(8 + channel_low, HALF, stride=16), :] = imag[:, lanes] * amplitude
    copies = []
    rows = HALF * 4
    for piece in range(4):
        part = pl.ds(piece * rows, rows)
        rounded[part, :] = scratch[part, :].astype(jnp.bfloat16)
        copies.append(pltpu.make_async_copy(rounded.at[part], out_ref.at[part], sems.at[piece]))
        copies[-1].start()
    for copy in copies:
        copy.wait()


def swap_table():
    r = np.arange(4 * LANES)[:, None]
    c = np.arange(4 * LANES)[None, :]
    same = (r % 32 == c % 32) & (r // 32 % 4 == c // 128) & (r // 128 == c // 32 % 4)
    return same.astype(np.float32).astype(jnp.bfloat16)


def flip_table():
    return np.eye(LANES, dtype=np.float32)[::-1].astype(jnp.bfloat16)


def cross_kernel(received_ref, swap_ref, flip_ref, out_ref, window, own):
    window[CHANNELS:, :] = jnp.zeros((OFFS, 2 * LANES), jnp.bfloat16)
    swap = swap_ref[...]
    group = 16
    for first in range(0, TILES, group):
        side_by_side = jnp.concatenate(
            [received_ref[first : first + group, block].reshape(group * 16, LANES) for block in range(4)], axis=1
        )
        swapped = product(side_by_side, swap)
        for tile in range(group):
            for part in range(2):
                eight = swapped[tile * 16 + part * 8 : tile * 16 + part * 8 + 8]
                rows = jnp.concatenate([eight[:, high * LANES : (high + 1) * LANES] for high in range(4)], axis=0)
                start = (first + tile) * 32
                window[start : start + 32, part * LANES : (part + 1) * LANES] = rows.astype(jnp.bfloat16)

    flip = flip_ref[...]
    for block in range(CHANNELS // LANES):
        turned = product(flip, window[block * LANES : (block + 1) * LANES, :])
        real, imag = turned[:, :LANES], turned[:, LANES:]
        own[block, :LANES] = jnp.concatenate([real, imag], axis=1).astype(jnp.bfloat16)
        own[block, LANES:] = jnp.concatenate([imag, -real], axis=1).astype(jnp.bfloat16)

    for block in range(CHANNELS // LANES):
        start = block * LANES
        both_parts = product_nt(own[block], window[start : start + LANES + OFFS, :])
        for part in range(2):
            cross = both_parts[part * LANES : (part + 1) * LANES]
            cross = pltpu.roll(cross, OFFS, 1, stride=1, stride_axis=0)
            for place in range(16):
                eight = cross[8 * place : 8 * place + 8]
                halves = jnp.concatenate([eight[:, :LANES], eight[:, LANES : 2 * LANES]], axis=0)
                out_ref[block * 16 + 15 - place, part] = halves.astype(jnp.bfloat16)


def lag_kernel(received_ref, table_ref, out_ref, wide, lags, sems):
    wide[...] = received_ref[...].astype(jnp.float32)
    table = table_ref[...]
    copies = []
    for channel in range(8):
        columns = []
        for upper in range(2):
            first = upper * 8 + 7 - channel
            real = wide[pl.ds(first, HALF, stride=32), :]
            imag = wide[pl.ds(16 + first, HALF, stride=32), :]
            columns.append(jnp.concatenate([real, imag], axis=0).astype(jnp.bfloat16))
        both = jnp.concatenate(columns, axis=1)
        lags[channel] = lax.dot_general(
            both, table, (((0,), (0,)), ((), ())), preferred_element_type=jnp.float32
        ).astype(jnp.bfloat16)
        if channel % 2:
            pair = pl.ds(channel - 1, 2)
            copies.append(pltpu.make_async_copy(lags.at[pair], out_ref.at[pair], sems.at[channel // 2]))
            copies[-1].start()
    for copy in copies:
        copy.wait()


def call(kernel, shape, scratch, vmem_mib, **specs):
    return pl.pallas_call(
        kernel,
        out_shape=jax.ShapeDtypeStruct(shape, jnp.bfloat16),
        scratch_shapes=scratch,
        compiler_params=pltpu.CompilerParams(vmem_limit_bytes=vmem_mib * MIB),
        **specs,
    )


def body(traces, live_flags):
    vmem = pl.BlockSpec(memory_space=pltpu.VMEM)
    whitened = call(
        whiten_kernel,
        (HALF * 16, LANES),
        [
            pltpu.VMEM((HALF * 16, LANES), jnp.float32),
            pltpu.VMEM((HALF * 16, LANES), jnp.bfloat16),
            pltpu.SemaphoreType.DMA((4,)),
        ],
        63,
        in_specs=[pl.BlockSpec(memory_space=pltpu.SMEM), vmem, vmem],
        out_specs=pl.BlockSpec(memory_space=pltpu.HBM),
    )(live_flags, traces.reshape(4, 8, 32, NFFT), jnp.asarray(dft_table_t()))
    one_bin = lax.all_to_all(whitened.reshape(HALF, 16, LANES), AXES, 0, 0, tiled=True)

    cross = call(
        cross_kernel,
        (HALF, 2, 16, LANES),
        [
            pltpu.VMEM((CHANNELS + OFFS, 2 * LANES), jnp.bfloat16),
            pltpu.VMEM((CHANNELS // LANES, 2 * LANES, 2 * LANES), jnp.bfloat16),
        ],
        40,
    )(one_bin.reshape(TILES, 4, 16, LANES), jnp.asarray(swap_table()), jnp.asarray(flip_table()))
    all_bins = lax.all_to_all(cross.reshape(HALF, 32, LANES), AXES, 0, 0, tiled=True)

    return call(
        lag_kernel,
        (8, OFFS, LAGS),
        [
            pltpu.VMEM((HALF * 32, LANES), jnp.float32),
            pltpu.VMEM((8, OFFS, LAGS), jnp.bfloat16),
            pltpu.SemaphoreType.DMA((4,)),
        ],
        40,
        in_specs=[vmem, vmem],
        out_specs=pl.BlockSpec(memory_space=pltpu.HBM),
    )(all_bins.reshape(HALF * 32, LANES), jnp.asarray(lag_table()))


def solution(mesh):
    return jax.shard_map(
        body,
        mesh=mesh,
        in_specs=(P(("row", "col"), "tm", None), P(("row", "col"))),
        out_specs=P(AXES, None, None),
        check_vma=False,
    )
```

```python
import jax
import jax.numpy as jnp
import numpy as np
from jax import lax
from jax.experimental import pallas as pl
from jax.experimental.pallas import tpu as pltpu
from jax.sharding import PartitionSpec as P

NFFT = 512
LANES = 128
HALF = 256
OFFS = 256
LAGS = 256
SMOOTH = 32
AXES = ("row", "col", "tm")
GROUP_AXES = ("col", "tm")
GROUP = 64
BINS = HALF // GROUP
ROW = 512
HALF_BLOCKS = ROW // 2 // LANES
MIB = 1024 * 1024


def dft_table_t():
    n = np.arange(NFFT, dtype=np.float64)[None, :]
    k = np.arange(HALF, dtype=np.float64)[:, None]
    taper = 0.5 - 0.5 * np.cos(2.0 * np.pi * n / NFFT)
    phase = 2.0 * np.pi * np.mod(n * k, NFFT) / NFFT
    return np.concatenate([taper * np.cos(phase), -taper * np.sin(phase)], axis=0).astype(jnp.bfloat16)


def lag_table():
    k = np.arange(HALF, dtype=np.float64)[:, None]
    t = (np.arange(LAGS) - LAGS // 2).astype(np.float64)[None, :]
    weight = np.where(k == 0, 1.0, 2.0) / NFFT
    phase = 2.0 * np.pi * np.mod(k * t, NFFT) / NFFT
    return np.concatenate([weight * np.cos(phase), -weight * np.sin(phase)], axis=0).astype(jnp.bfloat16)


def zero_one(shape, holds):
    row = lax.broadcasted_iota(jnp.int32, shape, 0)
    column = lax.broadcasted_iota(jnp.int32, shape, 1)
    return jnp.where(holds(row, column), 1.0, 0.0).astype(jnp.bfloat16)


def product(left, right):
    return jnp.dot(left, right, preferred_element_type=jnp.float32)


def product_nt(left, right):
    return lax.dot_general(left, right, (((1,), (1,)), ((), ())), preferred_element_type=jnp.float32)


def whiten_kernel(flags_ref, traces_ref, table_ref, out_ref, scratch, rounded, sems):
    band = zero_one((HALF, 2 * HALF), lambda r, c: jnp.abs(r - c % HALF) <= SMOOTH)
    bin_index = lax.broadcasted_iota(jnp.int32, (HALF, LANES), 0)
    count = jnp.minimum(bin_index + SMOOTH, HALF - 1) - jnp.maximum(bin_index - SMOOTH, 0) + 1
    inverse = 1.0 / count.astype(jnp.float32)
    lane_block = lax.broadcasted_iota(jnp.int32, (1, LANES), 1) // 32
    table = table_ref[...]
    width = 8
    for start in range(0, 8, width):
        rows = jnp.concatenate(
            [traces_ref[high, start + low] for low in range(width) for high in range(4)], axis=0
        )
        spectra = product_nt(table, rows)
        real, imag = spectra[:HALF], spectra[HALF:]
        power = real * real + imag * imag
        power_high = power.astype(jnp.bfloat16)
        power_low = (power - power_high.astype(jnp.float32)).astype(jnp.bfloat16)
        total = product(band, jnp.concatenate([power_high, power_low], axis=0))
        for low in range(width):
            lanes = slice(low * LANES, (low + 1) * LANES)
            channel_low = start + low
            live = jnp.zeros((1, LANES), jnp.float32)
            for high in range(4):
                live = jnp.where(lane_block == high, flags_ref[high * 8 + channel_low].astype(jnp.float32), live)
            amplitude = live * lax.rsqrt(total[:, lanes] * inverse + 1e-06)
            scratch[pl.ds(channel_low, HALF, stride=16), :] = real[:, lanes] * amplitude
            scratch[pl.ds(8 + channel_low, HALF, stride=16), :] = imag[:, lanes] * amplitude
    copies = []
    rows = HALF * 4
    for piece in range(4):
        part = pl.ds(piece * rows, rows)
        rounded[part, :] = scratch[part, :].astype(jnp.bfloat16)
        copies.append(pltpu.make_async_copy(rounded.at[part], out_ref.at[part], sems.at[piece]))
        copies[-1].start()
    for copy in copies:
        copy.wait()


def swap_table():
    r = np.arange(4 * LANES)[:, None]
    c = np.arange(4 * LANES)[None, :]
    same = (r % 32 == c % 32) & (r // 32 % 4 == c // 128) & (r // 128 == c // 32 % 4)
    return same.astype(np.float32).astype(jnp.bfloat16)


def flip_table():
    return np.eye(LANES, dtype=np.float32)[::-1].astype(jnp.bfloat16)


def place_tiles(received_ref, swap, index, window, first_row):
    tiles = received_ref.shape[0]
    side_by_side = jnp.concatenate(
        [received_ref[:, block, index].reshape(tiles * 16, LANES) for block in range(4)], axis=1
    )
    swapped = product(side_by_side, swap)
    for tile in range(tiles):
        for part in range(2):
            eight = swapped[tile * 16 + part * 8 : tile * 16 + part * 8 + 8]
            rows = jnp.concatenate([eight[:, high * LANES : (high + 1) * LANES] for high in range(4)], axis=0)
            start = first_row + tile * 32
            window[index, start : start + 32, part * LANES : (part + 1) * LANES] = rows.astype(jnp.bfloat16)


def turn_blocks(window, flip, index, own):
    for block in range(own.shape[1]):
        turned = product(flip, window[index, block * LANES : (block + 1) * LANES, :])
        real, imag = turned[:, :LANES], turned[:, LANES:]
        own[index, block, :LANES] = jnp.concatenate([real, imag], axis=1).astype(jnp.bfloat16)
        own[index, block, LANES:] = jnp.concatenate([imag, -real], axis=1).astype(jnp.bfloat16)


def cross_block(own, others, index, block, out_ref):
    both_parts = product_nt(own, others)
    for part in range(2):
        cross = both_parts[part * LANES : (part + 1) * LANES]
        cross = pltpu.roll(cross, OFFS, 1, stride=1, stride_axis=0)
        for place in range(16):
            eight = cross[8 * place : 8 * place + 8]
            halves = jnp.concatenate([eight[:, :LANES], eight[:, LANES : 2 * LANES]], axis=0)
            out_ref[block * 16 + 15 - place, index, part] = halves.astype(jnp.bfloat16)


def near_kernel(received_ref, swap_ref, flip_ref, out_ref, window, own):
    swap = swap_ref[...]
    flip = flip_ref[...]
    for index in range(BINS):
        place_tiles(received_ref, swap, index, window, 0)
    for index in range(BINS):
        turn_blocks(window, flip, index, own)
    for index in range(BINS):
        for block in range(HALF_BLOCKS):
            start = block * LANES
            cross_block(own[index, block], window[index, start : start + LANES + OFFS], index, block, out_ref)


def far_kernel(halo_ref, window_ref, own_ref, swap_ref, near_ref, out_ref, beyond):
    swap = swap_ref[...]
    for index in range(BINS):
        place_tiles(halo_ref, swap, index, beyond, 0)
    out_ref[: ROW // 2 // 8] = near_ref[...]
    for index in range(BINS):
        for block in range(HALF_BLOCKS, 2 * HALF_BLOCKS):
            start = block * LANES
            others = jnp.concatenate(
                [window_ref[index, start:], beyond[index, : start + LANES + OFFS - ROW]], axis=0
            )
            cross_block(own_ref[index, block], others, index, block, out_ref)


def lag_kernel(received_ref, table_ref, out_ref, lags, sems):
    table = table_ref[...]
    copies = []
    for channel in range(8):
        columns = []
        for upper in range(2):
            first = upper * 8 + 7 - channel
            real = received_ref[pl.ds(first, HALF, stride=32), :]
            imag = received_ref[pl.ds(16 + first, HALF, stride=32), :]
            columns.append(jnp.concatenate([real, imag], axis=0))
        both = jnp.concatenate(columns, axis=1)
        lags[channel] = lax.dot_general(
            both, table, (((0,), (0,)), ((), ())), preferred_element_type=jnp.float32
        ).astype(jnp.bfloat16)
        if channel % 2:
            pair = pl.ds(channel - 1, 2)
            copies.append(pltpu.make_async_copy(lags.at[pair], out_ref.at[pair], sems.at[channel // 2]))
            copies[-1].start()
    for copy in copies:
        copy.wait()


def call(kernel, shape, scratch, vmem_mib, **options):
    return pl.pallas_call(
        kernel,
        out_shape=jax.tree.map(lambda s: jax.ShapeDtypeStruct(s, jnp.bfloat16), shape, is_leaf=lambda s: isinstance(s, tuple)),
        scratch_shapes=scratch,
        compiler_params=pltpu.CompilerParams(vmem_limit_bytes=vmem_mib * MIB),
        **options,
    )


def body(traces, live_flags):
    vmem = pl.BlockSpec(memory_space=pltpu.VMEM)
    hbm = pl.BlockSpec(memory_space=pltpu.HBM)
    whitened = call(
        whiten_kernel,
        (HALF * 16, LANES),
        [
            pltpu.VMEM((HALF * 16, LANES), jnp.float32),
            pltpu.VMEM((HALF * 16, LANES), jnp.bfloat16),
            pltpu.SemaphoreType.DMA((4,)),
        ],
        63,
        in_specs=[pl.BlockSpec(memory_space=pltpu.SMEM), vmem, vmem],
        out_specs=hbm,
    )(live_flags, traces.reshape(4, 8, 32, NFFT), jnp.asarray(dft_table_t()))
    some_bins = lax.all_to_all(whitened.reshape(GROUP, BINS, 16, LANES), GROUP_AXES, 0, 0, tiled=True)
    some_bins = some_bins.reshape(ROW // 32, 4, BINS, 16, LANES)

    first = some_bins[: OFFS // 32]
    halo = lax.ppermute(first, "row", [(1, 0), (2, 1), (3, 2)])
    swap, flip = jnp.asarray(swap_table()), jnp.asarray(flip_table())
    near, window, own = call(
        near_kernel,
        [
            (GROUP // 2, BINS, 2, 16, LANES),
            (BINS, ROW, 2 * LANES),
            (BINS, 2 * HALF_BLOCKS, 2 * LANES, 2 * LANES),
        ],
        [],
        32,
    )(some_bins, swap, flip)
    cross = call(
        far_kernel,
        (GROUP, BINS, 2, 16, LANES),
        [pltpu.VMEM((BINS, OFFS, 2 * LANES), jnp.bfloat16)],
        32,
    )(halo, window, own, swap, near)
    all_bins = lax.all_to_all(cross.reshape(GROUP, BINS * 32, LANES), GROUP_AXES, 0, 0, tiled=True)

    return call(
        lag_kernel,
        (8, OFFS, LAGS),
        [pltpu.VMEM((8, OFFS, LAGS), jnp.bfloat16), pltpu.SemaphoreType.DMA((4,))],
        32,
        in_specs=[vmem, vmem],
        out_specs=hbm,
    )(all_bins.reshape(HALF * 32, LANES), jnp.asarray(lag_table()))


def solution(mesh):
    return jax.shard_map(
        body,
        mesh=mesh,
        in_specs=(P(("row", "col"), "tm", None), P(("row", "col"))),
        out_specs=P(AXES, None, None),
        check_vma=False,
    )
```

```python
import jax
import jax.numpy as jnp
import numpy as np
from jax import lax
from jax.experimental import pallas as pl
from jax.experimental.pallas import tpu as pltpu
from jax.sharding import PartitionSpec as P

NFFT = 512
LANES = 128
HALF = 256
OFFS = 256
LAGS = 256
SMOOTH = 32
AXES = ("row", "col", "tm")
GROUP_AXES = ("col", "tm")
GROUP = 64
BINS = HALF // GROUP
ROW = 512
HALF_BLOCKS = ROW // 2 // LANES
MIB = 1024 * 1024


def dft_table_t():
    n = np.arange(NFFT, dtype=np.float64)[None, :]
    k = np.arange(HALF, dtype=np.float64)[:, None]
    taper = 0.5 - 0.5 * np.cos(2.0 * np.pi * n / NFFT)
    phase = 2.0 * np.pi * np.mod(n * k, NFFT) / NFFT
    return np.concatenate([taper * np.cos(phase), -taper * np.sin(phase)], axis=0).astype(jnp.bfloat16)


def lag_table():
    k = np.arange(HALF, dtype=np.float64)[:, None]
    t = (np.arange(LAGS) - LAGS // 2).astype(np.float64)[None, :]
    weight = np.where(k == 0, 1.0, 2.0) / NFFT
    phase = 2.0 * np.pi * np.mod(k * t, NFFT) / NFFT
    return np.concatenate([weight * np.cos(phase), -weight * np.sin(phase)], axis=0).astype(jnp.bfloat16)


def zero_one(shape, holds):
    row = lax.broadcasted_iota(jnp.int32, shape, 0)
    column = lax.broadcasted_iota(jnp.int32, shape, 1)
    return jnp.where(holds(row, column), 1.0, 0.0).astype(jnp.bfloat16)


def product(left, right):
    return jnp.dot(left, right, preferred_element_type=jnp.float32)


def product_nt(left, right):
    return lax.dot_general(left, right, (((1,), (1,)), ((), ())), preferred_element_type=jnp.float32)


def whiten_kernel(flags_ref, traces_ref, table_ref, out_ref, scratch, rounded, sems):
    band = zero_one((HALF, 2 * HALF), lambda r, c: jnp.abs(r - c % HALF) <= SMOOTH)
    bin_index = lax.broadcasted_iota(jnp.int32, (HALF, LANES), 0)
    count = jnp.minimum(bin_index + SMOOTH, HALF - 1) - jnp.maximum(bin_index - SMOOTH, 0) + 1
    inverse = 1.0 / count.astype(jnp.float32)
    lane_block = lax.broadcasted_iota(jnp.int32, (1, LANES), 1) // 32
    table = table_ref[...]
    width = 8
    for start in range(0, 8, width):
        rows = jnp.concatenate(
            [traces_ref[high, start + low] for low in range(width) for high in range(4)], axis=0
        )
        spectra = product_nt(table, rows)
        real, imag = spectra[:HALF], spectra[HALF:]
        power = real * real + imag * imag
        power_high = power.astype(jnp.bfloat16)
        power_low = (power - power_high.astype(jnp.float32)).astype(jnp.bfloat16)
        total = product(band, jnp.concatenate([power_high, power_low], axis=0))
        for low in range(width):
            lanes = slice(low * LANES, (low + 1) * LANES)
            channel_low = start + low
            live = jnp.zeros((1, LANES), jnp.float32)
            for high in range(4):
                live = jnp.where(lane_block == high, flags_ref[high * 8 + channel_low].astype(jnp.float32), live)
            amplitude = live * lax.rsqrt(total[:, lanes] * inverse + 1e-06)
            scratch[channel_low] = (real[:, lanes] * amplitude).astype(jnp.bfloat16)
            scratch[8 + channel_low] = (imag[:, lanes] * amplitude).astype(jnp.bfloat16)
    copies = []
    rows = HALF * 4
    for piece in range(4):
        part = pl.ds(piece * rows, rows)
        for first in range(piece * HALF // 4, (piece + 1) * HALF // 4, 16):
            block = jnp.swapaxes(scratch[:, first : first + 16, :], 0, 1)
            rounded[first * 16 : (first + 16) * 16, :] = block.reshape(HALF, LANES)
        copies.append(pltpu.make_async_copy(rounded.at[part], out_ref.at[part], sems.at[piece]))
        copies[-1].start()
    for copy in copies:
        copy.wait()


def swap_table():
    r = np.arange(4 * LANES)[:, None]
    c = np.arange(4 * LANES)[None, :]
    same = (r % 32 == c % 32) & (r // 32 % 4 == c // 128) & (r // 128 == c // 32 % 4)
    return same.astype(np.float32).astype(jnp.bfloat16)


def flip_table():
    return np.eye(LANES, dtype=np.float32)[::-1].astype(jnp.bfloat16)


def place_tiles(received_ref, swap, index, window, first_row):
    tiles = received_ref.shape[0]
    side_by_side = jnp.concatenate(
        [received_ref[:, block, index].reshape(tiles * 16, LANES) for block in range(4)], axis=1
    )
    swapped = product(side_by_side, swap)
    for tile in range(tiles):
        for part in range(2):
            eight = swapped[tile * 16 + part * 8 : tile * 16 + part * 8 + 8]
            rows = jnp.concatenate([eight[:, high * LANES : (high + 1) * LANES] for high in range(4)], axis=0)
            start = first_row + tile * 32
            window[index, start : start + 32, part * LANES : (part + 1) * LANES] = rows.astype(jnp.bfloat16)


def turn_blocks(window, flip, index, own):
    for block in range(own.shape[1]):
        turned = product(flip, window[index, block * LANES : (block + 1) * LANES, :])
        real, imag = turned[:, :LANES], turned[:, LANES:]
        own[index, block, :LANES] = jnp.concatenate([real, imag], axis=1).astype(jnp.bfloat16)
        own[index, block, LANES:] = jnp.concatenate([imag, -real], axis=1).astype(jnp.bfloat16)


def cross_block(own, others, index, block, out_ref):
    both_parts = product_nt(own, others)
    for part in range(2):
        cross = both_parts[part * LANES : (part + 1) * LANES]
        cross = pltpu.roll(cross, OFFS, 1, stride=1, stride_axis=0)
        for place in range(16):
            eight = cross[8 * place : 8 * place + 8]
            halves = jnp.concatenate([eight[:, :LANES], eight[:, LANES : 2 * LANES]], axis=0)
            out_ref[block * 16 + 15 - place, index, part] = halves.astype(jnp.bfloat16)


def near_kernel(received_ref, swap_ref, flip_ref, out_ref, window, own):
    swap = swap_ref[...]
    flip = flip_ref[...]
    for index in range(BINS):
        place_tiles(received_ref, swap, index, window, 0)
    for index in range(BINS):
        turn_blocks(window, flip, index, own)
    for index in range(BINS):
        for block in range(HALF_BLOCKS):
            start = block * LANES
            cross_block(own[index, block], window[index, start : start + LANES + OFFS], index, block, out_ref)


def far_kernel(halo_ref, window_ref, own_ref, swap_ref, near_ref, out_ref, beyond):
    swap = swap_ref[...]
    for index in range(BINS):
        place_tiles(halo_ref, swap, index, beyond, 0)
    out_ref[: ROW // 2 // 8] = near_ref[...]
    for index in range(BINS):
        for block in range(HALF_BLOCKS, 2 * HALF_BLOCKS):
            start = block * LANES
            others = jnp.concatenate(
                [window_ref[index, start:], beyond[index, : start + LANES + OFFS - ROW]], axis=0
            )
            cross_block(own_ref[index, block], others, index, block, out_ref)


def lag_kernel(received_ref, table_ref, out_ref, by_row, lags, sems):
    group = 16
    for first in range(0, HALF, group):
        block = received_ref[first * 32 : (first + group) * 32, :].reshape(group, 32, LANES)
        by_row[:, first : first + group, :] = jnp.swapaxes(block, 0, 1)
    table = table_ref[...]
    copies = []
    for channel in range(8):
        columns = []
        for upper in range(2):
            first = upper * 8 + 7 - channel
            columns.append(jnp.concatenate([by_row[first], by_row[16 + first]], axis=0))
        both = jnp.concatenate(columns, axis=1)
        lags[channel] = lax.dot_general(
            both, table, (((0,), (0,)), ((), ())), preferred_element_type=jnp.float32
        ).astype(jnp.bfloat16)
        if channel % 2:
            pair = pl.ds(channel - 1, 2)
            copies.append(pltpu.make_async_copy(lags.at[pair], out_ref.at[pair], sems.at[channel // 2]))
            copies[-1].start()
    for copy in copies:
        copy.wait()


def call(kernel, shape, scratch, vmem_mib, **options):
    return pl.pallas_call(
        kernel,
        out_shape=jax.tree.map(lambda s: jax.ShapeDtypeStruct(s, jnp.bfloat16), shape, is_leaf=lambda s: isinstance(s, tuple)),
        scratch_shapes=scratch,
        compiler_params=pltpu.CompilerParams(vmem_limit_bytes=vmem_mib * MIB),
        **options,
    )


def body(traces, live_flags):
    vmem = pl.BlockSpec(memory_space=pltpu.VMEM)
    hbm = pl.BlockSpec(memory_space=pltpu.HBM)
    whitened = call(
        whiten_kernel,
        (HALF * 16, LANES),
        [
            pltpu.VMEM((16, HALF, LANES), jnp.bfloat16),
            pltpu.VMEM((HALF * 16, LANES), jnp.bfloat16),
            pltpu.SemaphoreType.DMA((4,)),
        ],
        63,
        in_specs=[pl.BlockSpec(memory_space=pltpu.SMEM), vmem, vmem],
        out_specs=hbm,
    )(live_flags, traces.reshape(4, 8, 32, NFFT), jnp.asarray(dft_table_t()))
    some_bins = lax.all_to_all(whitened.reshape(GROUP, BINS, 16, LANES), GROUP_AXES, 0, 0, tiled=True)
    some_bins = some_bins.reshape(ROW // 32, 4, BINS, 16, LANES)

    first = some_bins[: OFFS // 32]
    halo = lax.ppermute(first, "row", [(1, 0), (2, 1), (3, 2)])
    swap, flip = jnp.asarray(swap_table()), jnp.asarray(flip_table())
    near, window, own = call(
        near_kernel,
        [
            (GROUP // 2, BINS, 2, 16, LANES),
            (BINS, ROW, 2 * LANES),
            (BINS, 2 * HALF_BLOCKS, 2 * LANES, 2 * LANES),
        ],
        [],
        32,
    )(some_bins, swap, flip)
    cross = call(
        far_kernel,
        (GROUP, BINS, 2, 16, LANES),
        [pltpu.VMEM((BINS, OFFS, 2 * LANES), jnp.bfloat16)],
        32,
    )(halo, window, own, swap, near)
    all_bins = lax.all_to_all(cross.reshape(GROUP, BINS * 32, LANES), GROUP_AXES, 0, 0, tiled=True)

    return call(
        lag_kernel,
        (8, OFFS, LAGS),
        [
            pltpu.VMEM((32, HALF, LANES), jnp.bfloat16),
            pltpu.VMEM((8, OFFS, LAGS), jnp.bfloat16),
            pltpu.SemaphoreType.DMA((4,)),
        ],
        32,
        in_specs=[vmem, vmem],
        out_specs=hbm,
    )(all_bins.reshape(HALF * 32, LANES), jnp.asarray(lag_table()))


def solution(mesh):
    return jax.shard_map(
        body,
        mesh=mesh,
        in_specs=(P(("row", "col"), "tm", None), P(("row", "col"))),
        out_specs=P(AXES, None, None),
        check_vma=False,
    )
```

```python
import jax
import jax.numpy as jnp
import numpy as np
from jax import lax
from jax.experimental import pallas as pl
from jax.experimental.pallas import tpu as pltpu
from jax.sharding import PartitionSpec as P

NFFT = 512
LANES = 128
HALF = 256
OFFS = 256
LAGS = 256
SMOOTH = 32
AXES = ("row", "col", "tm")
GROUP_AXES = ("col", "tm")
GROUP = 64
BINS = HALF // GROUP
ROW = 512
HALF_BLOCKS = ROW // 2 // LANES
MIB = 1024 * 1024


def dft_table_t():
    n = np.arange(NFFT, dtype=np.float64)[None, :]
    k = np.arange(HALF, dtype=np.float64)[:, None]
    taper = 0.5 - 0.5 * np.cos(2.0 * np.pi * n / NFFT)
    phase = 2.0 * np.pi * np.mod(n * k, NFFT) / NFFT
    return np.concatenate([taper * np.cos(phase), -taper * np.sin(phase)], axis=0).astype(jnp.bfloat16)


def lag_table():
    k = np.arange(HALF, dtype=np.float64)[:, None]
    t = (np.arange(LAGS) - LAGS // 2).astype(np.float64)[None, :]
    weight = np.where(k == 0, 1.0, 2.0) / NFFT
    phase = 2.0 * np.pi * np.mod(k * t, NFFT) / NFFT
    return np.concatenate([weight * np.cos(phase), -weight * np.sin(phase)], axis=0).astype(jnp.bfloat16)


def zero_one(shape, holds):
    row = lax.broadcasted_iota(jnp.int32, shape, 0)
    column = lax.broadcasted_iota(jnp.int32, shape, 1)
    return jnp.where(holds(row, column), 1.0, 0.0).astype(jnp.bfloat16)


def product(left, right):
    return jnp.dot(left, right, preferred_element_type=jnp.float32)


def product_nt(left, right):
    return lax.dot_general(left, right, (((1,), (1,)), ((), ())), preferred_element_type=jnp.float32)


def whiten_kernel(flags_ref, traces_ref, table_ref, out_ref, scratch, rounded, sems):
    band = zero_one((HALF, 2 * HALF), lambda r, c: jnp.abs(r - c % HALF) <= SMOOTH)
    bin_index = lax.broadcasted_iota(jnp.int32, (HALF, LANES), 0)
    count = jnp.minimum(bin_index + SMOOTH, HALF - 1) - jnp.maximum(bin_index - SMOOTH, 0) + 1
    inverse = 1.0 / count.astype(jnp.float32)
    lane_block = lax.broadcasted_iota(jnp.int32, (1, LANES), 1) // 32
    table = table_ref[...]
    width = 4
    for start in range(0, 8, width):
        rows = jnp.concatenate(
            [traces_ref[high, start + low] for low in range(width) for high in range(4)], axis=0
        )
        spectra = product_nt(table, rows)
        real, imag = spectra[:HALF], spectra[HALF:]
        power = real * real + imag * imag
        power_high = power.astype(jnp.bfloat16)
        power_low = (power - power_high.astype(jnp.float32)).astype(jnp.bfloat16)
        total = product(band, jnp.concatenate([power_high, power_low], axis=0))
        for low in range(width):
            lanes = slice(low * LANES, (low + 1) * LANES)
            channel_low = start + low
            live = jnp.zeros((1, LANES), jnp.float32)
            for high in range(4):
                live = jnp.where(lane_block == high, flags_ref[high * 8 + channel_low].astype(jnp.float32), live)
            amplitude = live * lax.rsqrt(total[:, lanes] * inverse + 1e-06)
            scratch[channel_low] = (real[:, lanes] * amplitude).astype(jnp.bfloat16)
            scratch[8 + channel_low] = (imag[:, lanes] * amplitude).astype(jnp.bfloat16)
    copies = []
    rows = HALF * 4
    for piece in range(4):
        part = pl.ds(piece * rows, rows)
        for first in range(piece * HALF // 4, (piece + 1) * HALF // 4, 16):
            block = jnp.swapaxes(scratch[:, first : first + 16, :], 0, 1)
            rounded[first * 16 : (first + 16) * 16, :] = block.reshape(HALF, LANES)
        copies.append(pltpu.make_async_copy(rounded.at[part], out_ref.at[part], sems.at[piece]))
        copies[-1].start()
    for copy in copies:
        copy.wait()


def swap_table():
    r = np.arange(4 * LANES)[:, None]
    c = np.arange(4 * LANES)[None, :]
    same = (r % 32 == c % 32) & (r // 32 % 4 == c // 128) & (r // 128 == c // 32 % 4)
    return same.astype(np.float32).astype(jnp.bfloat16)


def flip_table():
    return np.eye(LANES, dtype=np.float32)[::-1].astype(jnp.bfloat16)


def place_tiles(received_ref, swap, index, window, first_row):
    tiles = received_ref.shape[0]
    side_by_side = jnp.concatenate(
        [received_ref[:, block, index].reshape(tiles * 16, LANES) for block in range(4)], axis=1
    )
    swapped = product(side_by_side, swap)
    for tile in range(tiles):
        for part in range(2):
            eight = swapped[tile * 16 + part * 8 : tile * 16 + part * 8 + 8]
            rows = jnp.concatenate([eight[:, high * LANES : (high + 1) * LANES] for high in range(4)], axis=0)
            start = first_row + tile * 32
            window[index, start : start + 32, part * LANES : (part + 1) * LANES] = rows.astype(jnp.bfloat16)


def turn_blocks(window, flip, index, own):
    for block in range(own.shape[1]):
        turned = product(flip, window[index, block * LANES : (block + 1) * LANES, :])
        real, imag = turned[:, :LANES], turned[:, LANES:]
        own[index, block, :LANES] = jnp.concatenate([real, imag], axis=1).astype(jnp.bfloat16)
        own[index, block, LANES:] = jnp.concatenate([imag, -real], axis=1).astype(jnp.bfloat16)


def cross_block(own, others, index, block, out_ref):
    both_parts = product_nt(own, others)
    for part in range(2):
        cross = both_parts[part * LANES : (part + 1) * LANES]
        cross = pltpu.roll(cross, OFFS, 1, stride=1, stride_axis=0)
        for place in range(16):
            eight = cross[8 * place : 8 * place + 8]
            halves = jnp.concatenate([eight[:, :LANES], eight[:, LANES : 2 * LANES]], axis=0)
            out_ref[block * 16 + 15 - place, index, part] = halves.astype(jnp.bfloat16)


def near_kernel(received_ref, swap_ref, flip_ref, out_ref, window, own):
    swap = swap_ref[...]
    flip = flip_ref[...]
    for index in range(BINS):
        place_tiles(received_ref, swap, index, window, 0)
    for index in range(BINS):
        turn_blocks(window, flip, index, own)
    for index in range(BINS):
        for block in range(HALF_BLOCKS):
            start = block * LANES
            cross_block(own[index, block], window[index, start : start + LANES + OFFS], index, block, out_ref)


def far_kernel(halo_ref, window_ref, own_ref, swap_ref, near_ref, out_ref, beyond):
    swap = swap_ref[...]
    for index in range(BINS):
        place_tiles(halo_ref, swap, index, beyond, 0)
    out_ref[: ROW // 2 // 8] = near_ref[...]
    for index in range(BINS):
        for block in range(HALF_BLOCKS, 2 * HALF_BLOCKS):
            start = block * LANES
            others = jnp.concatenate(
                [window_ref[index, start:], beyond[index, : start + LANES + OFFS - ROW]], axis=0
            )
            cross_block(own_ref[index, block], others, index, block, out_ref)


def lag_kernel(received_ref, table_ref, out_ref, by_row, lags, sems):
    group = 16
    for first in range(0, HALF, group):
        block = received_ref[first * 32 : (first + group) * 32, :].reshape(group, 32, LANES)
        by_row[:, first : first + group, :] = jnp.swapaxes(block, 0, 1)
    table = table_ref[...]
    copies = []
    for channel in range(8):
        columns = []
        for upper in range(2):
            first = upper * 8 + 7 - channel
            columns.append(jnp.concatenate([by_row[first], by_row[16 + first]], axis=0))
        both = jnp.concatenate(columns, axis=1)
        lags[channel] = lax.dot_general(
            both, table, (((0,), (0,)), ((), ())), preferred_element_type=jnp.float32
        ).astype(jnp.bfloat16)
        if channel % 2:
            pair = pl.ds(channel - 1, 2)
            copies.append(pltpu.make_async_copy(lags.at[pair], out_ref.at[pair], sems.at[channel // 2]))
            copies[-1].start()
    for copy in copies:
        copy.wait()


def call(kernel, shape, scratch, vmem_mib, **options):
    return pl.pallas_call(
        kernel,
        out_shape=jax.tree.map(lambda s: jax.ShapeDtypeStruct(s, jnp.bfloat16), shape, is_leaf=lambda s: isinstance(s, tuple)),
        scratch_shapes=scratch,
        compiler_params=pltpu.CompilerParams(vmem_limit_bytes=vmem_mib * MIB),
        **options,
    )


def body(traces, live_flags):
    vmem = pl.BlockSpec(memory_space=pltpu.VMEM)
    hbm = pl.BlockSpec(memory_space=pltpu.HBM)
    whitened = call(
        whiten_kernel,
        (HALF * 16, LANES),
        [
            pltpu.VMEM((16, HALF, LANES), jnp.bfloat16),
            pltpu.VMEM((HALF * 16, LANES), jnp.bfloat16),
            pltpu.SemaphoreType.DMA((4,)),
        ],
        63,
        in_specs=[pl.BlockSpec(memory_space=pltpu.SMEM), vmem, vmem],
        out_specs=hbm,
    )(live_flags, traces.reshape(4, 8, 32, NFFT), jnp.asarray(dft_table_t()))
    some_bins = lax.all_to_all(whitened.reshape(GROUP, BINS, 16, LANES), GROUP_AXES, 0, 0, tiled=True)
    some_bins = some_bins.reshape(ROW // 32, 4, BINS, 16, LANES)

    first = some_bins[: OFFS // 32]
    halo = lax.ppermute(first, "row", [(1, 0), (2, 1), (3, 2)])
    swap, flip = jnp.asarray(swap_table()), jnp.asarray(flip_table())
    near, window, own = call(
        near_kernel,
        [
            (GROUP // 2, BINS, 2, 16, LANES),
            (BINS, ROW, 2 * LANES),
            (BINS, 2 * HALF_BLOCKS, 2 * LANES, 2 * LANES),
        ],
        [],
        32,
    )(some_bins, swap, flip)
    cross = call(
        far_kernel,
        (GROUP, BINS, 2, 16, LANES),
        [pltpu.VMEM((BINS, OFFS, 2 * LANES), jnp.bfloat16)],
        32,
    )(halo, window, own, swap, near)
    all_bins = lax.all_to_all(cross.reshape(GROUP, BINS * 32, LANES), GROUP_AXES, 0, 0, tiled=True)

    return call(
        lag_kernel,
        (8, OFFS, LAGS),
        [
            pltpu.VMEM((32, HALF, LANES), jnp.bfloat16),
            pltpu.VMEM((8, OFFS, LAGS), jnp.bfloat16),
            pltpu.SemaphoreType.DMA((4,)),
        ],
        32,
        in_specs=[vmem, vmem],
        out_specs=hbm,
    )(all_bins.reshape(HALF * 32, LANES), jnp.asarray(lag_table()))


def solution(mesh):
    return jax.shard_map(
        body,
        mesh=mesh,
        in_specs=(P(("row", "col"), "tm", None), P(("row", "col"))),
        out_specs=P(AXES, None, None),
        check_vma=False,
    )
```

```python
import jax
import jax.numpy as jnp
import numpy as np
from jax import lax
from jax.experimental import pallas as pl
from jax.experimental.pallas import tpu as pltpu
from jax.sharding import PartitionSpec as P

NFFT = 512
LANES = 128
HALF = 256
OFFS = 256
LAGS = 256
SMOOTH = 32
AXES = ("row", "col", "tm")
GROUP_AXES = ("col", "tm")
GROUP = 64
BINS = HALF // GROUP
ROW = 512
MIB = 1024 * 1024


def dft_table_t():
    n = np.arange(NFFT, dtype=np.float64)[None, :]
    k = np.arange(HALF, dtype=np.float64)[:, None]
    taper = 0.5 - 0.5 * np.cos(2.0 * np.pi * n / NFFT)
    phase = 2.0 * np.pi * np.mod(n * k, NFFT) / NFFT
    return np.concatenate([taper * np.cos(phase), -taper * np.sin(phase)], axis=0).astype(jnp.bfloat16)


def lag_table():
    k = np.arange(HALF, dtype=np.float64)[:, None]
    t = (np.arange(LAGS) - LAGS // 2).astype(np.float64)[None, :]
    weight = np.where(k == 0, 1.0, 2.0) / NFFT
    phase = 2.0 * np.pi * np.mod(k * t, NFFT) / NFFT
    return np.concatenate([weight * np.cos(phase), -weight * np.sin(phase)], axis=0).astype(jnp.bfloat16)


def zero_one(shape, holds):
    row = lax.broadcasted_iota(jnp.int32, shape, 0)
    column = lax.broadcasted_iota(jnp.int32, shape, 1)
    return jnp.where(holds(row, column), 1.0, 0.0).astype(jnp.bfloat16)


def product(left, right):
    return jnp.dot(left, right, preferred_element_type=jnp.float32)


def product_nt(left, right):
    return lax.dot_general(left, right, (((1,), (1,)), ((), ())), preferred_element_type=jnp.float32)


def whiten_kernel(flags_ref, traces_ref, table_ref, out_ref, scratch, rounded, sems):
    band = zero_one((HALF, 2 * HALF), lambda r, c: jnp.abs(r - c % HALF) <= SMOOTH)
    bin_index = lax.broadcasted_iota(jnp.int32, (HALF, LANES), 0)
    count = jnp.minimum(bin_index + SMOOTH, HALF - 1) - jnp.maximum(bin_index - SMOOTH, 0) + 1
    inverse = 1.0 / count.astype(jnp.float32)
    lane_block = lax.broadcasted_iota(jnp.int32, (1, LANES), 1) // 32
    table = table_ref[...]
    width = 8
    for start in range(0, 8, width):
        rows = jnp.concatenate(
            [traces_ref[high, start + low] for low in range(width) for high in range(4)], axis=0
        )
        spectra = product_nt(table, rows)
        real, imag = spectra[:HALF], spectra[HALF:]
        power = real * real + imag * imag
        power_high = power.astype(jnp.bfloat16)
        power_low = (power - power_high.astype(jnp.float32)).astype(jnp.bfloat16)
        total = product(band, jnp.concatenate([power_high, power_low], axis=0))
        for low in range(width):
            lanes = slice(low * LANES, (low + 1) * LANES)
            channel_low = start + low
            live = jnp.zeros((1, LANES), jnp.float32)
            for high in range(4):
                live = jnp.where(lane_block == high, flags_ref[high * 8 + channel_low].astype(jnp.float32), live)
            amplitude = live * lax.rsqrt(total[:, lanes] * inverse + 1e-06)
            scratch[channel_low] = (real[:, lanes] * amplitude).astype(jnp.bfloat16)
            scratch[8 + channel_low] = (imag[:, lanes] * amplitude).astype(jnp.bfloat16)
    copies = []
    rows = HALF * 4
    for piece in range(4):
        part = pl.ds(piece * rows, rows)
        for first in range(piece * HALF // 4, (piece + 1) * HALF // 4, 16):
            block = jnp.swapaxes(scratch[:, first : first + 16, :], 0, 1)
            rounded[first * 16 : (first + 16) * 16, :] = block.reshape(HALF, LANES)
        copies.append(pltpu.make_async_copy(rounded.at[part], out_ref.at[part], sems.at[piece]))
        copies[-1].start()
    for copy in copies:
        copy.wait()


def swap_table():
    r = np.arange(4 * LANES)[:, None]
    c = np.arange(4 * LANES)[None, :]
    same = (r % 32 == c % 32) & (r // 32 % 4 == c // 128) & (r // 128 == c // 32 % 4)
    return same.astype(np.float32).astype(jnp.bfloat16)


def flip_table():
    return np.eye(LANES, dtype=np.float32)[::-1].astype(jnp.bfloat16)


def place_tiles(received_ref, swap, index, window, first_row):
    tiles = received_ref.shape[0]
    side_by_side = jnp.concatenate(
        [received_ref[:, block, index].reshape(tiles * 16, LANES) for block in range(4)], axis=1
    )
    swapped = product(side_by_side, swap)
    for tile in range(tiles):
        for part in range(2):
            eight = swapped[tile * 16 + part * 8 : tile * 16 + part * 8 + 8]
            rows = jnp.concatenate([eight[:, high * LANES : (high + 1) * LANES] for high in range(4)], axis=0)
            start = first_row + tile * 32
            window[index, start : start + 32, part * LANES : (part + 1) * LANES] = rows.astype(jnp.bfloat16)


def turn_blocks(window, flip, index, own):
    for block in range(own.shape[1]):
        turned = product(flip, window[index, block * LANES : (block + 1) * LANES, :])
        real, imag = turned[:, :LANES], turned[:, LANES:]
        own[index, block, :LANES] = jnp.concatenate([real, imag], axis=1).astype(jnp.bfloat16)
        own[index, block, LANES:] = jnp.concatenate([imag, -real], axis=1).astype(jnp.bfloat16)


def skewed(factors, others):
    both_parts = product_nt(factors, others)
    shift = both_parts.shape[1] - LANES
    return [
        pltpu.roll(both_parts[part * LANES : (part + 1) * LANES], shift, 1, stride=1, stride_axis=0)
        for part in range(2)
    ]


def store_half(parts, half, out_ref, block, index, upper):
    lanes = slice(half * LANES, (half + 1) * LANES)
    for place in range(16):
        rows = slice(8 * place, 8 * place + 8)
        both = jnp.concatenate([part[rows, lanes] for part in parts], axis=0)
        out_ref[block * 16 + 15 - place, index, upper] = both.astype(jnp.bfloat16)


def near_kernel(received_ref, swap_ref, flip_ref, out_ref, window, own):
    swap = swap_ref[...]
    flip = flip_ref[...]
    for index in range(BINS):
        place_tiles(received_ref, swap, index, window, 0)
    for index in range(BINS):
        turn_blocks(window, flip, index, own)
    for index in range(BINS):
        for block in range(3):
            reach = min(3, 4 - block)
            start = block * LANES
            parts = skewed(own[index, block], window[index, start : start + reach * LANES])
            for half in range(reach - 1):
                store_half(parts, half, out_ref, block, index, half)


def far_kernel(halo_ref, window_ref, own_ref, swap_ref, near_ref, out_ref, beyond):
    swap = swap_ref[...]
    for index in range(BINS):
        place_tiles(halo_ref, swap, index, beyond, 0)
    out_ref[:32] = near_ref[:32]
    out_ref[32:48, :, 0] = near_ref[32:48, :, 0]
    for index in range(BINS):
        tail = window_ref[index, 3 * LANES :]
        parts = skewed(own_ref[index, 2], jnp.concatenate([tail, beyond[index, :LANES]], axis=0))
        store_half(parts, 0, out_ref, 2, index, 1)
        parts = skewed(own_ref[index, 3], jnp.concatenate([tail, beyond[index]], axis=0))
        for half in range(2):
            store_half(parts, half, out_ref, 3, index, half)


def lag_kernel(received_ref, table_ref, out_ref, by_row, lags, sems):
    group = 16
    for first in range(0, HALF, group):
        block = received_ref[first * 32 : (first + group) * 32, :].reshape(group, 32, LANES)
        by_row[:, first : first + group, :] = jnp.swapaxes(block, 0, 1)
    table = table_ref[...]
    copies = []
    for channel in range(8):
        columns = []
        for upper in range(2):
            first = upper * 16 + 7 - channel
            columns.append(jnp.concatenate([by_row[first], by_row[8 + first]], axis=0))
        both = jnp.concatenate(columns, axis=1)
        lags[channel] = lax.dot_general(
            both, table, (((0,), (0,)), ((), ())), preferred_element_type=jnp.float32
        ).astype(jnp.bfloat16)
        if channel % 2:
            pair = pl.ds(channel - 1, 2)
            copies.append(pltpu.make_async_copy(lags.at[pair], out_ref.at[pair], sems.at[channel // 2]))
            copies[-1].start()
    for copy in copies:
        copy.wait()


def call(kernel, shape, scratch, vmem_mib, **options):
    return pl.pallas_call(
        kernel,
        out_shape=jax.tree.map(lambda s: jax.ShapeDtypeStruct(s, jnp.bfloat16), shape, is_leaf=lambda s: isinstance(s, tuple)),
        scratch_shapes=scratch,
        compiler_params=pltpu.CompilerParams(vmem_limit_bytes=vmem_mib * MIB),
        **options,
    )


def body(traces, live_flags):
    vmem = pl.BlockSpec(memory_space=pltpu.VMEM)
    hbm = pl.BlockSpec(memory_space=pltpu.HBM)
    whitened = call(
        whiten_kernel,
        (HALF * 16, LANES),
        [
            pltpu.VMEM((16, HALF, LANES), jnp.bfloat16),
            pltpu.VMEM((HALF * 16, LANES), jnp.bfloat16),
            pltpu.SemaphoreType.DMA((4,)),
        ],
        63,
        in_specs=[pl.BlockSpec(memory_space=pltpu.SMEM), vmem, vmem],
        out_specs=hbm,
    )(live_flags, traces.reshape(4, 8, 32, NFFT), jnp.asarray(dft_table_t()))
    some_bins = lax.all_to_all(whitened.reshape(GROUP, BINS, 16, LANES), GROUP_AXES, 0, 0, tiled=True)
    some_bins = some_bins.reshape(ROW // 32, 4, BINS, 16, LANES)

    first = some_bins[: OFFS // 32]
    halo = lax.ppermute(first, "row", [(1, 0), (2, 1), (3, 2)])
    swap, flip = jnp.asarray(swap_table()), jnp.asarray(flip_table())
    near, window, own = call(
        near_kernel,
        [
            (48, BINS, 2, 16, LANES),
            (BINS, ROW, 2 * LANES),
            (BINS, ROW // LANES, 2 * LANES, 2 * LANES),
        ],
        [],
        32,
    )(some_bins, swap, flip)
    cross = call(
        far_kernel,
        (GROUP, BINS, 2, 16, LANES),
        [pltpu.VMEM((BINS, OFFS, 2 * LANES), jnp.bfloat16)],
        32,
    )(halo, window, own, swap, near)
    all_bins = lax.all_to_all(cross.reshape(GROUP, BINS * 32, LANES), GROUP_AXES, 0, 0, tiled=True)

    return call(
        lag_kernel,
        (8, OFFS, LAGS),
        [
            pltpu.VMEM((32, HALF, LANES), jnp.bfloat16),
            pltpu.VMEM((8, OFFS, LAGS), jnp.bfloat16),
            pltpu.SemaphoreType.DMA((4,)),
        ],
        32,
        in_specs=[vmem, vmem],
        out_specs=hbm,
    )(all_bins.reshape(HALF * 32, LANES), jnp.asarray(lag_table()))


def solution(mesh):
    return jax.shard_map(
        body,
        mesh=mesh,
        in_specs=(P(("row", "col"), "tm", None), P(("row", "col"))),
        out_specs=P(AXES, None, None),
        check_vma=False,
    )
```

```python
import jax
import jax.numpy as jnp
import numpy as np
from jax import lax
from jax.experimental import pallas as pl
from jax.experimental.pallas import tpu as pltpu
from jax.sharding import PartitionSpec as P

NFFT = 512
LANES = 128
HALF = 256
OFFS = 256
LAGS = 256
SMOOTH = 32
AXES = ("row", "col", "tm")
GROUP_AXES = ("col", "tm")
GROUP = 64
BINS = HALF // GROUP
ROW = 512
HALF_BLOCKS = ROW // 2 // LANES
MIB = 1024 * 1024


def dft_table_t():
    n = np.arange(NFFT, dtype=np.float64)[None, :]
    k = np.arange(HALF, dtype=np.float64)[:, None]
    taper = 0.5 - 0.5 * np.cos(2.0 * np.pi * n / NFFT)
    phase = 2.0 * np.pi * np.mod(n * k, NFFT) / NFFT
    return np.concatenate([taper * np.cos(phase), -taper * np.sin(phase)], axis=0).astype(jnp.bfloat16)


def lag_table():
    k = np.arange(HALF, dtype=np.float64)[:, None]
    t = (np.arange(LAGS) - LAGS // 2).astype(np.float64)[None, :]
    weight = np.where(k == 0, 1.0, 2.0) / NFFT
    phase = 2.0 * np.pi * np.mod(k * t, NFFT) / NFFT
    return np.concatenate([weight * np.cos(phase), -weight * np.sin(phase)], axis=0).astype(jnp.bfloat16)


def zero_one(shape, holds):
    row = lax.broadcasted_iota(jnp.int32, shape, 0)
    column = lax.broadcasted_iota(jnp.int32, shape, 1)
    return jnp.where(holds(row, column), 1.0, 0.0).astype(jnp.bfloat16)


def product(left, right):
    return jnp.dot(left, right, preferred_element_type=jnp.float32)


def product_nt(left, right):
    return lax.dot_general(left, right, (((1,), (1,)), ((), ())), preferred_element_type=jnp.float32)


def whiten_kernel(flags_ref, traces_ref, table_ref, out_ref, scratch, rounded, sems):
    band = zero_one((HALF, 2 * HALF), lambda r, c: jnp.abs(r - c % HALF) <= SMOOTH)
    bin_index = lax.broadcasted_iota(jnp.int32, (HALF, LANES), 0)
    count = jnp.minimum(bin_index + SMOOTH, HALF - 1) - jnp.maximum(bin_index - SMOOTH, 0) + 1
    inverse = 1.0 / count.astype(jnp.float32)
    lane_block = lax.broadcasted_iota(jnp.int32, (1, LANES), 1) // 32
    table = table_ref[...]
    width = 8
    for start in range(0, 8, width):
        rows = jnp.concatenate(
            [traces_ref[high, start + low] for low in range(width) for high in range(4)], axis=0
        )
        spectra = product_nt(table, rows)
        real, imag = spectra[:HALF], spectra[HALF:]
        power = real * real + imag * imag
        power_high = power.astype(jnp.bfloat16)
        power_low = (power - power_high.astype(jnp.float32)).astype(jnp.bfloat16)
        total = product(band, jnp.concatenate([power_high, power_low], axis=0))
        for low in range(width):
            lanes = slice(low * LANES, (low + 1) * LANES)
            channel_low = start + low
            live = jnp.zeros((1, LANES), jnp.float32)
            for high in range(4):
                live = jnp.where(lane_block == high, flags_ref[high * 8 + channel_low].astype(jnp.float32), live)
            amplitude = live * lax.rsqrt(total[:, lanes] * inverse + 1e-06)
            scratch[channel_low] = (real[:, lanes] * amplitude).astype(jnp.bfloat16)
            scratch[8 + channel_low] = (imag[:, lanes] * amplitude).astype(jnp.bfloat16)
    copies = []
    rows = HALF * 4
    for piece in range(4):
        part = pl.ds(piece * rows, rows)
        for first in range(piece * HALF // 4, (piece + 1) * HALF // 4, 16):
            block = jnp.swapaxes(scratch[:, first : first + 16, :], 0, 1)
            rounded[first * 16 : (first + 16) * 16, :] = block.reshape(HALF, LANES)
        copies.append(pltpu.make_async_copy(rounded.at[part], out_ref.at[part], sems.at[piece]))
        copies[-1].start()
    for copy in copies:
        copy.wait()


def swap_table():
    r = np.arange(4 * LANES)[:, None]
    c = np.arange(4 * LANES)[None, :]
    same = (r % 32 == c % 32) & (r // 32 % 4 == c // 128) & (r // 128 == c // 32 % 4)
    return same.astype(np.float32).astype(jnp.bfloat16)


def flip_table():
    return np.eye(LANES, dtype=np.float32)[::-1].astype(jnp.bfloat16)


def place_tiles(received_ref, swap, index, window, first_row):
    tiles = received_ref.shape[0]
    side_by_side = jnp.concatenate(
        [received_ref[:, block, index].reshape(tiles * 16, LANES) for block in range(4)], axis=1
    )
    swapped = product(side_by_side, swap)
    for tile in range(tiles):
        for part in range(2):
            eight = swapped[tile * 16 + part * 8 : tile * 16 + part * 8 + 8]
            rows = jnp.concatenate([eight[:, high * LANES : (high + 1) * LANES] for high in range(4)], axis=0)
            start = first_row + tile * 32
            window[index, start : start + 32, part * LANES : (part + 1) * LANES] = rows.astype(jnp.bfloat16)


def turn_blocks(window, flip, index, own):
    for block in range(own.shape[1]):
        turned = product(flip, window[index, block * LANES : (block + 1) * LANES, :])
        real, imag = turned[:, :LANES], turned[:, LANES:]
        own[index, block, :LANES] = jnp.concatenate([real, imag], axis=1).astype(jnp.bfloat16)
        own[index, block, LANES:] = jnp.concatenate([imag, -real], axis=1).astype(jnp.bfloat16)


def cross_block(own, others, index, block, out_ref):
    both_parts = product_nt(own, others)
    for part in range(2):
        cross = both_parts[part * LANES : (part + 1) * LANES]
        cross = pltpu.roll(cross, OFFS, 1, stride=1, stride_axis=0)
        for place in range(16):
            eight = cross[8 * place : 8 * place + 8]
            halves = jnp.concatenate([eight[:, :LANES], eight[:, LANES : 2 * LANES]], axis=0)
            out_ref[block * 16 + 15 - place, index, part] = halves.astype(jnp.bfloat16)


def near_kernel(received_ref, swap_ref, flip_ref, out_ref, window, own):
    swap = swap_ref[...]
    flip = flip_ref[...]
    for index in range(BINS):
        place_tiles(received_ref, swap, index, window, 0)
    for index in range(BINS):
        turn_blocks(window, flip, index, own)
    for index in range(BINS):
        for block in range(HALF_BLOCKS):
            start = block * LANES
            cross_block(own[index, block], window[index, start : start + LANES + OFFS], index, block, out_ref)


def far_kernel(far_ref, chip_ref, window_ref, own_ref, swap_ref, near_ref, out_ref, halo_ref, beyond):
    halo_ref[...] = far_ref[...] + chip_ref[...]
    swap = swap_ref[...]
    for index in range(BINS):
        place_tiles(halo_ref, swap, index, beyond, 0)
    out_ref[: ROW // 2 // 8] = near_ref[...]
    for index in range(BINS):
        for block in range(HALF_BLOCKS, 2 * HALF_BLOCKS):
            start = block * LANES
            others = jnp.concatenate(
                [window_ref[index, start:], beyond[index, : start + LANES + OFFS - ROW]], axis=0
            )
            cross_block(own_ref[index, block], others, index, block, out_ref)


def lag_kernel(received_ref, table_ref, out_ref, by_row, lags, sems):
    group = 16
    for first in range(0, HALF, group):
        block = received_ref[first * 32 : (first + group) * 32, :].reshape(group, 32, LANES)
        by_row[:, first : first + group, :] = jnp.swapaxes(block, 0, 1)
    table = table_ref[...]
    copies = []
    for channel in range(8):
        columns = []
        for upper in range(2):
            first = upper * 8 + 7 - channel
            columns.append(jnp.concatenate([by_row[first], by_row[16 + first]], axis=0))
        both = jnp.concatenate(columns, axis=1)
        lags[channel] = lax.dot_general(
            both, table, (((0,), (0,)), ((), ())), preferred_element_type=jnp.float32
        ).astype(jnp.bfloat16)
        if channel % 2:
            pair = pl.ds(channel - 1, 2)
            copies.append(pltpu.make_async_copy(lags.at[pair], out_ref.at[pair], sems.at[channel // 2]))
            copies[-1].start()
    for copy in copies:
        copy.wait()


def call(kernel, shape, scratch, vmem_mib, **options):
    return pl.pallas_call(
        kernel,
        out_shape=jax.tree.map(lambda s: jax.ShapeDtypeStruct(s, jnp.bfloat16), shape, is_leaf=lambda s: isinstance(s, tuple)),
        scratch_shapes=scratch,
        compiler_params=pltpu.CompilerParams(vmem_limit_bytes=vmem_mib * MIB),
        **options,
    )


def body(traces, live_flags):
    vmem = pl.BlockSpec(memory_space=pltpu.VMEM)
    hbm = pl.BlockSpec(memory_space=pltpu.HBM)
    whitened = call(
        whiten_kernel,
        (HALF * 16, LANES),
        [
            pltpu.VMEM((16, HALF, LANES), jnp.bfloat16),
            pltpu.VMEM((HALF * 16, LANES), jnp.bfloat16),
            pltpu.SemaphoreType.DMA((4,)),
        ],
        63,
        in_specs=[pl.BlockSpec(memory_space=pltpu.SMEM), vmem, vmem],
        out_specs=hbm,
    )(live_flags, traces.reshape(4, 8, 32, NFFT), jnp.asarray(dft_table_t()))
    some_bins = lax.all_to_all(whitened.reshape(GROUP, BINS, 16, LANES), GROUP_AXES, 0, 0, tiled=True)
    some_bins = some_bins.reshape(ROW // 32, 4, BINS, 16, LANES)

    first = some_bins[: OFFS // 32]
    far_halo = lax.ppermute(first, "row", [(2, 1)])
    chip_halo = lax.ppermute(first, "row", [(1, 0), (3, 2)])
    swap, flip = jnp.asarray(swap_table()), jnp.asarray(flip_table())
    near, window, own = call(
        near_kernel,
        [
            (GROUP // 2, BINS, 2, 16, LANES),
            (BINS, ROW, 2 * LANES),
            (BINS, 2 * HALF_BLOCKS, 2 * LANES, 2 * LANES),
        ],
        [],
        32,
    )(some_bins, swap, flip)
    cross = call(
        far_kernel,
        (GROUP, BINS, 2, 16, LANES),
        [
            pltpu.VMEM((OFFS // 32, 4, BINS, 16, LANES), jnp.bfloat16),
            pltpu.VMEM((BINS, OFFS, 2 * LANES), jnp.bfloat16),
        ],
        32,
    )(far_halo, chip_halo, window, own, swap, near)
    all_bins = lax.all_to_all(cross.reshape(GROUP, BINS * 32, LANES), GROUP_AXES, 0, 0, tiled=True)

    return call(
        lag_kernel,
        (8, OFFS, LAGS),
        [
            pltpu.VMEM((32, HALF, LANES), jnp.bfloat16),
            pltpu.VMEM((8, OFFS, LAGS), jnp.bfloat16),
            pltpu.SemaphoreType.DMA((4,)),
        ],
        32,
        in_specs=[vmem, vmem],
        out_specs=hbm,
    )(all_bins.reshape(HALF * 32, LANES), jnp.asarray(lag_table()))


def solution(mesh):
    return jax.shard_map(
        body,
        mesh=mesh,
        in_specs=(P(("row", "col"), "tm", None), P(("row", "col"))),
        out_specs=P(AXES, None, None),
        check_vma=False,
    )
```
